256 devices in a mesh: depth: 8 (over y, core), row: 4 (over z_lo), col: 8 (over x, z_hi).
Axes of the slice: x: 4, y: 4, z: 8 (z_hi: 2, z_lo: 4; z = z_hi * 4 + z_lo), core: 2. Of those that a mesh axis runs over, the one named last changes fastest.
Arguments:
- inputs: bfloat16 [8, 512, 16384], P('col', None, ('depth', 'row')), may hold values from -6 to 6
- qweight: bfloat16 [16384, 9216], P(('depth', 'col'), 'row'), may hold values from -0.046875 to 0.046875
- scales: float32 [128, 72], P(('depth', 'col'), 'row'), may hold values from 0.25 to 4, as said below
- grad_out: bfloat16 [8, 512, 9216], P('col', 'depth', 'row'), may hold values from -0.796875 to 0.796875
Outputs:
- projected: bfloat16 [8, 512, 9216], P('col', 'depth', 'row')
- grad_inputs: bfloat16 [8, 512, 16384], P('col', None, ('depth', 'row'))
- grad_weight: bfloat16 [16384, 9216], P(('depth', 'col'), 'row')
The draws below stay inside these ranges and needn't reach their ends.
Inputs may be any that keep to these rules, and one draw needn't show every extreme that they name: `scales`: every scale is a power of two.
All inputs are finite; a program needn't handle non-finite values.
Results may differ from the reference program's by a relative error of at most 0.019.
Values may be sent and summed in bfloat16 or wider, within the bound.
No kernel may reach another device: no remote copies, remote signals or barrier semaphores. Data moves between devices by JAX's collectives and lax.ppermute only.
A program may use at most 128 MiB of HBM per device.

```python
import jax
import jax.numpy as jnp

D = 16384
BLOCK = 128
ROWS = 512
F = 9216
SEQS = 8


def draw_scales(key, part):
    key = jax.random.fold_in(key, 7)
    picks = jax.random.randint(key, (D // BLOCK, F // BLOCK), 0, 5)
    table = jnp.array([0.25, 0.5, 1.0, 2.0, 4.0], jnp.float32)
    return jnp.take(table, picks)


def strengthened(drawn, own_key, source, target, blocks, factor):
    owner, partner = [(jnp.arange(drawn.shape[dim]) // (drawn.shape[dim] // blocks)).reshape([-1 if axis == dim else 1 for axis in range(drawn.ndim)]) for dim in (source, target)]
    chosen = jax.random.permutation(own_key, blocks)[partner]
    strong = (owner == chosen) | (owner == (partner + blocks // 2) % blocks)
    return jnp.where(strong, factor * drawn, drawn)


def levels(key, dims, split, smallest, largest):
    def one(axis_at, parts):
        draws = jax.random.uniform(jax.random.fold_in(jax.random.fold_in(key, 6), axis_at), (parts,), jnp.float32, smallest / len(split), largest / len(split))
        return jnp.repeat(jnp.exp(draws), dims[axis_at] // parts).reshape((-1,) + (1,) * (len(dims) - axis_at - 1))

    loudness = one(*split[0])
    for cut in split[1:]:
        loudness = loudness * one(*cut)
    return loudness


def normal_values(stream_key, dims, spread, most, pieces=(), kind=jnp.bfloat16):
    entries = spread * jax.random.normal(stream_key, dims, jnp.float32)
    if pieces:
        entries = entries * levels(stream_key, dims, pieces, -0.22, 0.18)
    return jnp.clip(entries, -most, most).astype(kind)


def gaussian_with(rng, dims, scale, most, pieces, heavy, kind=jnp.bfloat16):
    drawn = scale * jax.random.normal(rng, dims, jnp.float32)
    if pieces:
        drawn = drawn * levels(rng, dims, pieces, -0.22, 0.18)
    return jnp.clip(strengthened(drawn, jax.random.fold_in(rng, 3), *heavy), -most, most).astype(kind)


def setup_inputs(seed: int = 0) -> dict:
    arg_keys = jax.random.split(jax.random.key(seed), 5)
    inputs = gaussian_with(arg_keys[0], (SEQS, ROWS, D), 1.0, 6.0, ((0, 8), (2, 32)), (2, 1, 32, 2.75))
    qweight = normal_values(arg_keys[1], (D, F), D ** -0.5, 0.046875, ((0, 64), (1, 4)))
    scales = draw_scales(jax.random.fold_in(arg_keys[4], 71), 0)
    grad_out = normal_values(arg_keys[3], (SEQS, ROWS, F), 0.1, 0.796875, ((0, 8), (1, 8), (2, 4)))
    return {"inputs": inputs, "qweight": qweight, "scales": scales, "grad_out": grad_out}


def dequantize(qweight, scales):
    expand = jnp.repeat(jnp.repeat(scales, BLOCK, axis=0), BLOCK, axis=1)
    return (qweight.astype(jnp.float32) * expand).astype(jnp.bfloat16)


def reference(inputs, qweight, scales, grad_out):
    weight = dequantize(qweight, scales)
    flat_in = inputs.reshape(SEQS * ROWS, D)
    flat_grad = grad_out.reshape(SEQS * ROWS, F)
    projected = jnp.dot(flat_in, weight, preferred_element_type=jnp.float32).astype(jnp.bfloat16)
    grad_inputs = jnp.dot(flat_grad, weight.T, preferred_element_type=jnp.float32).astype(jnp.bfloat16)
    total = jnp.zeros((D, F), jnp.float32)
    for index in range(SEQS):
        partial_value = jnp.dot(inputs[index].T, grad_out[index], preferred_element_type=jnp.float32)
        total = total + partial_value.astype(jnp.bfloat16).astype(jnp.float32)
    return (projected.reshape(SEQS, ROWS, F), grad_inputs.reshape(SEQS, ROWS, D), total.astype(jnp.bfloat16))
```

```python
import jax
import jax.numpy as jnp
from jax import lax
from jax.experimental import pallas as pl
from jax.experimental.pallas import tpu as pltpu
from jax.sharding import Mesh, PartitionSpec as P

BLOCK = 128
BF = jnp.bfloat16
F32 = jnp.float32
VMEM_LIMIT = 56 * 1024 * 1024


def params():
    return pltpu.CompilerParams(vmem_limit_bytes=VMEM_LIMIT)


def cost(flops, moved):
    return pl.CostEstimate(flops=flops, bytes_accessed=moved, transcendentals=0)


def whole(shape):
    return pl.BlockSpec(shape, lambda *_: (0,) * len(shape))


SCALAR = pl.BlockSpec(memory_space=pltpu.SMEM)


def ring(size, step):
    return [(i, (i + step) % size) for i in range(size)]


def swapped(step):
    return [
        (zl * 2 + zh, ((zl + step) % 4) * 2 + 1 - zh)
        for zl in range(4)
        for zh in range(2)
    ]


def dequantize_kernel(scales, quantized, weight):
    for r in range(scales.shape[0]):
        for c in range(scales.shape[1]):
            at = (pl.ds(r * BLOCK, BLOCK), pl.ds(c * BLOCK, BLOCK))
            weight[at] = (quantized[at].astype(F32) * scales[r, c]).astype(BF)


def dequantize(quantized, scales):
    return pl.pallas_call(
        dequantize_kernel,
        out_shape=jax.ShapeDtypeStruct(quantized.shape, BF),
        in_specs=[SCALAR, whole(quantized.shape)],
        out_specs=whole(quantized.shape),
        compiler_params=params(),
        cost_estimate=cost(quantized.size, 4 * quantized.size),
    )(scales, quantized)


def forward_kernel(place, *refs):
    pieces, weights, (out, panel) = refs[:8], refs[8:12], refs[12:]
    turn, y, k = place[0], place[1], place[2]

    @pl.when(pl.program_id(0) == 0)
    def _():
        for s in range(2):
            for j in range(4):
                m = lax.rem(j + 4 - turn, 4)
                lanes = pl.ds(pl.multiple_of(m * 256, 256), 256)
                for b in range(8):
                    e = lax.rem(y - b // 2 + 4, 4)
                    kk = lax.rem(k + b % 2, 2)
                    row = kk * 512 + e * 128 + s * 64
                    rows = pl.ds(pl.multiple_of(row, 64), 64)
                    panel[rows, lanes] = pieces[s * 4 + j][b * 64 : b * 64 + 64, :]

    right = jnp.concatenate([w[...] for w in weights], axis=0)
    total = jnp.dot(panel[...], right, preferred_element_type=F32)
    out[...] = total.astype(BF)


def forward(place, pieces, weights):
    width = weights[0].shape[1]
    tile = 256
    return pl.pallas_call(
        forward_kernel,
        grid=(width // tile,),
        out_shape=jax.ShapeDtypeStruct((1024, width), BF),
        in_specs=[SCALAR]
        + [whole((512, 256))] * 8
        + [pl.BlockSpec((256, tile), lambda n: (0, n))] * 4,
        out_specs=pl.BlockSpec((1024, tile), lambda n: (0, n)),
        scratch_shapes=[pltpu.VMEM((1024, 1024), BF)],
        compiler_params=params(),
        cost_estimate=cost(2 * 1024 * 1024 * width, 2 * (1024 * 1024 + 2 * 1024 * width)),
    )(place, *pieces, *weights)


def weight_grad_kernel(place, *refs):
    pieces, grad, outs, panel = refs[:8], refs[8], refs[9:13], refs[13]
    turn = place[0]

    @pl.when(pl.program_id(0) == 0)
    def _():
        for s in range(2):
            for j in range(4):
                m = lax.rem(j + 4 - turn, 4)
                lanes = pl.ds(pl.multiple_of(m * 256, 256), 256)
                panel[s * 512 : s * 512 + 512, lanes] = pieces[s * 4 + j][...]

    total = lax.dot_general(
        panel[...], grad[...], (((0,), (0,)), ((), ())), preferred_element_type=F32
    )
    for m in range(4):
        outs[m][...] = total[m * 256 : m * 256 + 256, :].astype(BF)


def weight_grad(place, pieces, grad):
    width = grad.shape[1]
    tile = 256
    return pl.pallas_call(
        weight_grad_kernel,
        grid=(width // tile,),
        out_shape=[jax.ShapeDtypeStruct((256, width), BF)] * 4,
        in_specs=[SCALAR]
        + [whole((512, 256))] * 8
        + [pl.BlockSpec((1024, tile), lambda n: (0, n))],
        out_specs=[pl.BlockSpec((256, tile), lambda n: (0, n))] * 4,
        scratch_shapes=[pltpu.VMEM((1024, 1024), BF)],
        compiler_params=params(),
        cost_estimate=cost(2 * 1024 * 1024 * width, 2 * (1024 * 1024 + 2 * 1024 * width)),
    )(place, *pieces, grad)


def backward_kernel(place, grad, *refs):
    weights, outs = refs[:4], refs[4:12]
    turn = place[0]
    step = pl.program_id(0)
    half = pl.num_programs(0) // 2
    tile = grad.shape[0]
    rows = pl.ds(pl.multiple_of(lax.rem(step, half) * tile, tile), tile)
    for m in range(4):
        total = lax.dot_general(
            grad[...], weights[m][...], (((1,), (1,)), ((), ())),
            preferred_element_type=F32,
        ).astype(BF)
        target = lax.rem(turn + m, 4)
        for s in range(2):
            for j in range(4):
                @pl.when((step // half == s) & (target == j))
                def _():
                    outs[s * 4 + j][rows, :] = total


def backward(place, grad, weights):
    width = grad.shape[1]
    tile = 256
    return pl.pallas_call(
        backward_kernel,
        grid=(1024 // tile,),
        out_shape=[jax.ShapeDtypeStruct((512, 256), BF)] * 8,
        in_specs=[SCALAR, pl.BlockSpec((tile, width), lambda n: (n, 0))]
        + [whole((256, width))] * 4,
        out_specs=[whole((512, 256))] * 8,
        compiler_params=params(),
        cost_estimate=cost(2 * 1024 * 1024 * width, 2 * (1024 * 1024 + 2 * 1024 * width)),
    )(place, grad, *weights)


def added(*terms):
    total = terms[0].astype(F32)
    for term in terms[1:]:
        total = total + term.astype(F32)
    return total.astype(BF)


def per_device(inputs, qweight, scales, grad_out):
    y, k, zl = lax.axis_index("y"), lax.axis_index("k"), lax.axis_index("zl")
    x, zh = lax.axis_index("x"), lax.axis_index("zh")
    turn = lax.rem(zl - x + 4, 4)
    place = jnp.stack([turn, y, k, zh]).astype(jnp.int32)

    grad_own = grad_out[0]
    grad_other = lax.ppermute(grad_own, "zh", ring(2, 1))

    panel = inputs[0]
    half_own = lax.dynamic_slice(panel, (0, zh * 256), (512, 256))
    half_other = lax.dynamic_slice(panel, (0, (1 - zh) * 256), (512, 256))
    near = [half_own] + [lax.ppermute(half_own, "zl", ring(4, j)) for j in (1, 2, 3)]
    far = [lax.ppermute(half_other, ("zl", "zh"), swapped(j)) for j in range(4)]
    pieces = near + far

    weight = dequantize(qweight, scales)
    before = lax.ppermute(weight, "x", ring(4, 1))
    after = lax.ppermute(weight, "x", ring(4, -1))
    across = jnp.concatenate(
        [
            lax.ppermute(before[:128], "x", ring(4, 1)),
            lax.ppermute(after[128:], "x", ring(4, -1)),
        ],
        axis=0,
    )
    weights = [weight, before, across, after]

    both = jnp.stack([grad_own, grad_other])
    grads = lax.all_gather(both, ("y", "k"), axis=1, tiled=True).reshape(1024, -1)

    sums = backward(place, grads, weights)
    own = [sums[0]] + [lax.ppermute(sums[j], "zl", ring(4, -j)) for j in (1, 2, 3)]
    other = [lax.ppermute(sums[4 + j], ("zl", "zh"), swapped(-j)) for j in range(4)]
    own, other = added(*own), added(*other)
    low = jnp.where(zh == 0, own, other)
    high = jnp.where(zh == 0, other, own)
    grad_inputs = jnp.concatenate([low, high], axis=1)

    terms = weight_grad(place, pieces, grads)
    top = lax.ppermute(terms[2][:128], "x", ring(4, 1))
    bottom = lax.ppermute(terms[2][128:], "x", ring(4, -1))
    up = jnp.concatenate([added(terms[3][:128], top), terms[3][128:]], axis=0)
    down = jnp.concatenate([terms[1][:128], added(terms[1][128:], bottom)], axis=0)
    up = lax.ppermute(up, "x", ring(4, 1))
    down = lax.ppermute(down, "x", ring(4, -1))
    grad_weight = added(terms[0], up, down)

    product = forward(place, pieces, weights)
    mine = added(product[:512], lax.ppermute(product[512:], "k", ring(2, 1)))
    blocks = [mine[e * 128 : e * 128 + 128] for e in range(4)]
    top = lax.ppermute(blocks[2][:64], "y", ring(4, 1))
    bottom = lax.ppermute(blocks[2][64:], "y", ring(4, -1))
    up = jnp.concatenate([added(blocks[3][:64], top), blocks[3][64:]], axis=0)
    down = jnp.concatenate([blocks[1][:64], added(blocks[1][64:], bottom)], axis=0)
    up = lax.ppermute(up, "y", ring(4, 1))
    down = lax.ppermute(down, "y", ring(4, -1))
    last = added(blocks[0], up, down)
    projected = added(last[:64], lax.ppermute(last[64:], "zh", ring(2, 1)))

    return projected[None], grad_inputs[None], grad_weight


def solution(mesh):
    axes = Mesh(mesh.devices.reshape(4, 2, 4, 4, 2), ("y", "k", "zl", "x", "zh"))
    return jax.shard_map(
        per_device,
        mesh=axes,
        in_specs=(
            P(("x", "zh"), None, ("y", "k", "zl")),
            P(("y", "k", "x", "zh"), "zl"),
            P(("y", "k", "x", "zh"), "zl"),
            P(("x", "zh"), ("y", "k"), "zl"),
        ),
        out_specs=(
            P(("x", "zh"), ("y", "k"), "zl"),
            P(("x", "zh"), None, ("y", "k", "zl")),
            P(("y", "k", "x", "zh"), "zl"),
        ),
        check_vma=False,
    )
```

```python
import jax
import jax.numpy as jnp
from jax import lax
from jax.experimental import pallas as pl
from jax.experimental.pallas import tpu as pltpu
from jax.sharding import Mesh, PartitionSpec as P

BLOCK = 128
BF = jnp.bfloat16
F32 = jnp.float32
VMEM_LIMIT = 56 * 1024 * 1024


def params():
    return pltpu.CompilerParams(vmem_limit_bytes=VMEM_LIMIT)


def cost(flops, moved):
    return pl.CostEstimate(flops=flops, bytes_accessed=moved, transcendentals=0)


def whole(shape):
    return pl.BlockSpec(shape, lambda *_: (0,) * len(shape))


SCALAR = pl.BlockSpec(memory_space=pltpu.SMEM)
ANY = pl.BlockSpec(memory_space=pl.ANY)


def ring(size, step):
    return [(i, (i + step) % size) for i in range(size)]


def prepare_kernel(scales, quantized, inputs, grad, top, bottom, split, passed):
    passed[...] = grad[...]
    for r, half in enumerate((top, bottom)):
        for c in range(scales.shape[1]):
            lanes = pl.ds(c * BLOCK, BLOCK)
            block = quantized[pl.ds(r * BLOCK, BLOCK), lanes].astype(F32)
            half[:, lanes] = (block * scales[r, c]).astype(BF)
    for zh in range(2):
        for zl in range(4):
            split[zl * 2 + zh] = inputs[:, zh * 256 : zh * 256 + 256]


def prepare(scales, quantized, inputs, grad):
    half = (BLOCK, quantized.shape[1])
    return pl.pallas_call(
        prepare_kernel,
        out_shape=[
            jax.ShapeDtypeStruct(half, BF),
            jax.ShapeDtypeStruct(half, BF),
            jax.ShapeDtypeStruct((8, 512, 256), BF),
            jax.ShapeDtypeStruct(grad.shape, BF),
        ],
        in_specs=[SCALAR, whole(quantized.shape), whole(inputs.shape), whole(grad.shape)],
        out_specs=[whole(half), whole(half), whole((8, 512, 256)), whole(grad.shape)],
        compiler_params=params(),
        cost_estimate=cost(quantized.size, 8 * quantized.size),
    )(scales, quantized, inputs, grad)


PRODUCT = cost(1024 * 1024, 1024 * 1024)


def stacked(refs):
    return jnp.concatenate([ref[...] for ref in refs], axis=0)


def halves(top, bottom, top_up, up, down, bottom_down):
    first, second = pl.ds(0, BLOCK), pl.ds(BLOCK, BLOCK)
    return (
        top, bottom, top_up, up.at[second],
        up.at[first], down.at[second], down.at[first], bottom_down,
    )


def forward_kernel(place, _, panel, *refs):
    weights, (own, other, left) = halves(*refs[:6]), refs[6:]
    x, y, k, zh = place[0], place[1], place[2], place[3]

    @pl.when(pl.program_id(0) == 0)
    def _():
        for at in range(8):
            m = lax.rem(x - at // 2 + 4, 4)
            s = lax.rem(at % 2 + zh, 2)
            lanes = pl.ds(pl.multiple_of(m * 256, 256), 256)
            for b in range(8):
                e = lax.rem(y - b // 2 + 4, 4)
                kk = lax.rem(k + b % 2, 2)
                rows = pl.ds(pl.multiple_of(kk * 512 + e * 128 + s * 64, 64), 64)
                left[rows, lanes] = panel[at, b * 64 : b * 64 + 64, :]

    total = jnp.dot(left[...], stacked(weights), preferred_element_type=F32)
    own[...] = total[:512].astype(BF)
    other[...] = total[512:].astype(BF)


def forward(place, after, panel, weights):
    width = weights[0].shape[1]
    tile = width // 3
    return pl.pallas_call(
        forward_kernel,
        grid=(width // tile,),
        out_shape=[jax.ShapeDtypeStruct((512, width), BF)] * 2,
        in_specs=[SCALAR, ANY, whole(panel.shape)]
        + [pl.BlockSpec((w.shape[0], tile), lambda n: (0, n)) for w in weights],
        out_specs=[pl.BlockSpec((512, tile), lambda n: (0, n))] * 2,
        scratch_shapes=[pltpu.VMEM((1024, 1024), BF)],
        compiler_params=params(),
        cost_estimate=PRODUCT,
    )(place, after, panel, *weights)


def weight_grad_kernel(place, _, panel, near, mine, theirs, *refs):
    outs, left, right = refs[:5], refs[5], refs[6]
    x, y, k, zh = place[0], place[1], place[2], place[3]

    @pl.when(pl.program_id(0) == 0)
    def _():
        for at in range(8):
            m = lax.rem(x - at // 2 + 4, 4)
            s = lax.rem(at % 2 + zh, 2)
            rows = pl.ds(pl.multiple_of(m * 256, 256), 256)
            lanes = pl.ds(pl.multiple_of(s * 512, 512), 512)
            left[rows, lanes] = panel[at].T

    right[:512, :] = near[...]
    for e in range(4):
        for kk, source in enumerate((mine, theirs)):
            block = lax.rem(y - e + 4, 4) * 2 + lax.rem(k + kk, 2)
            rows = pl.ds(pl.multiple_of(512 + block * 64, 64), 64)
            right[rows, :] = source[e * 64 : e * 64 + 64, :]
    total = jnp.dot(left[...], right[...], preferred_element_type=F32)
    at = 0
    for out in outs:
        out[...] = total[at : at + out.shape[0]].astype(BF)
        at += out.shape[0]


def weight_grad(place, after, panel, near, mine, theirs):
    width = near.shape[1]
    tile = width // 3
    sizes = (256, 256, 128, 128, 256)
    return pl.pallas_call(
        weight_grad_kernel,
        grid=(width // tile,),
        out_shape=[jax.ShapeDtypeStruct((rows, width), BF) for rows in sizes],
        in_specs=[SCALAR, ANY, whole(panel.shape)]
        + [pl.BlockSpec((rows, tile), lambda n: (0, n)) for rows in (512, 256, 256)],
        out_specs=[pl.BlockSpec((rows, tile), lambda n: (0, n)) for rows in sizes],
        scratch_shapes=[pltpu.VMEM((1024, 1024), BF), pltpu.VMEM((1024, tile), BF)],
        compiler_params=params(),
        cost_estimate=PRODUCT,
    )(place, after, panel, near, mine, theirs)


def backward_kernel(place, _, near, mine, theirs, *refs):
    weights, out = halves(*refs[:6]), refs[6]
    x, y, k, zh = place[0], place[1], place[2], place[3]
    step = pl.program_id(0)
    rows = pl.ds(pl.multiple_of(step * 256, 256), 256)
    far = stacked((mine, theirs))
    for m in range(4):
        at = lax.rem(x - m + 4, 4) * 2
        right = stacked(weights[2 * m : 2 * m + 2])
        total = lax.dot_general(
            near[...], right, (((1,), (1,)), ((), ())), preferred_element_type=F32
        )
        out[at + zh, rows, :] = total.astype(BF)
        total = lax.dot_general(
            far, right, (((1,), (1,)), ((), ())), preferred_element_type=F32
        ).astype(BF)
        for i in range(4):
            block = lax.rem(y - 2 * step - i % 2 + 4, 4) * 2 + lax.rem(k + i // 2, 2)
            target = pl.ds(pl.multiple_of(block * 64, 64), 64)
            out[at + 1 - zh, target, :] = total[i * 64 : i * 64 + 64]


def backward(place, after, near, mine, theirs, weights):
    width = near.shape[1]
    return pl.pallas_call(
        backward_kernel,
        grid=(2,),
        out_shape=jax.ShapeDtypeStruct((8, 512, 256), BF),
        in_specs=[SCALAR, ANY]
        + [pl.BlockSpec((rows, width), lambda n: (n, 0)) for rows in (256, 128, 128)]
        + [whole(w.shape) for w in weights],
        out_specs=whole((8, 512, 256)),
        compiler_params=params(),
        cost_estimate=PRODUCT,
    )(place, after, near, mine, theirs, *weights)


def summed(*refs):
    total = refs[0].astype(F32)
    for ref in refs[1:]:
        total = total + ref.astype(F32)
    return total.astype(BF)


def local(kernel, outs, after, *args):
    after = after if isinstance(after, tuple) else (after,)
    moved = sum(2 * a.size for a in args) + sum(2 * a * b for a, b in outs)
    return pl.pallas_call(
        lambda *refs: kernel(*refs[len(after) :]),
        out_shape=[jax.ShapeDtypeStruct(shape, BF) for shape in outs],
        in_specs=[ANY] * len(after) + [whole(a.shape) for a in args],
        out_specs=[whole(shape) for shape in outs],
        compiler_params=params(),
        cost_estimate=cost(moved, moved),
    )(*after, *args)


def relay_kernel(grad, top, bottom, top_up, bottom_down, passed, up, down):
    passed[...] = grad[...]
    up[:BLOCK], up[BLOCK:] = top_up[...], bottom[...]
    down[:BLOCK], down[BLOCK:] = top[...], bottom_down[...]


def collect_kernel(here, up, across, down, out):
    at = 0
    for part in (here, up, across, down):
        out[pl.ds(at, part.shape[0]), :] = part[...]
        at += part.shape[0]


def pair_kernel(mine, theirs, *parts):
    at = 0
    for part in parts:
        rows = pl.ds(at, part.shape[0])
        part[...] = summed(mine[rows, :], theirs[rows, :])
        at += part.shape[0]


def onward_kernel(up, down, from_below, from_above, up_out, down_out):
    half = from_below.shape[0]
    up_out[:half] = summed(up[:half], from_below[...])
    up_out[half:] = up[half:]
    down_out[:half] = down[:half]
    down_out[half:] = summed(down[half:], from_above[...])


def finish_kernel(own, from_below, from_above, *outs):
    at = 0
    for out in outs:
        rows = pl.ds(at, out.shape[0])
        out[...] = summed(own[rows, :], from_below[rows, :], from_above[rows, :])
        at += out.shape[0]


def shift(array, axis, step):
    return lax.ppermute(array, axis, ring(lax.axis_size(axis), step))


def per_device(inputs, qweight, scales, grad_out):
    x, y, k, zh = (lax.axis_index(name) for name in ("x", "y", "k", "zh"))
    place = jnp.stack([x, y, k, zh]).astype(jnp.int32)
    F = qweight.shape[1]

    near = lax.all_gather(grad_out[0], ("y", "k"), axis=0, tiled=True)

    top, bottom, split, passed = prepare(scales, qweight, inputs[0], grad_out[0])
    panel = lax.all_to_all(split, ("zl", "zh"), 0, 0, tiled=True)

    top_up, bottom_down = shift(top, "x", 1), shift(bottom, "x", -1)
    far, up, down = local(
        relay_kernel,
        [passed.shape, (256, F), (256, F)],
        (),
        shift(passed, "zh", 1), top, bottom, top_up, bottom_down,
    )
    up, down = shift(up, "x", 1), shift(down, "x", -1)
    weights = (top, bottom, top_up, up, down, bottom_down)
    others = [shift(far, "y", e) for e in (1, 2, 3)]
    (mine,) = local(collect_kernel, [(256, F)], (), far, *others)
    theirs = shift(mine, "k", 1)

    sums = backward(place, mine, near, mine, theirs, weights)
    own, other = forward(place, sums, panel, weights)
    other = shift(other, "k", 1)
    terms = weight_grad(place, own, panel, near, mine, theirs)

    shapes = [(128, F), (128, F), (64, F), (64, F), (128, F)]
    here, down, top, bottom, up = local(pair_kernel, shapes, terms[0], own, other)
    top, bottom = shift(top, "y", 1), shift(bottom, "y", -1)
    up, down = local(onward_kernel, [(128, F)] * 2, here, up, down, top, bottom)
    up, down = shift(up, "y", 1), shift(down, "y", -1)
    mine, far = local(finish_kernel, [(64, F)] * 2, here, here, up, down)
    projected = summed(mine, shift(far, "zh", 1))

    sums = lax.all_to_all(sums, ("zl", "zh"), 0, 0, tiled=True)
    grad_inputs = jnp.concatenate(
        [summed(*[sums[zl * 2 + h] for zl in range(4)]) for h in range(2)], axis=1
    )

    here, down, top, bottom, up = terms
    top, bottom = shift(top, "x", 1), shift(bottom, "x", -1)
    up, down = local(onward_kernel, [(256, F)] * 2, up, up, down, top, bottom)
    up, down = shift(up, "x", 1), shift(down, "x", -1)
    (grad_weight,) = local(finish_kernel, [(256, F)], here, here, up, down)

    return projected[None], grad_inputs[None], grad_weight


def solution(mesh):
    axes = Mesh(mesh.devices.reshape(4, 2, 4, 4, 2), ("y", "k", "zl", "x", "zh"))
    return jax.shard_map(
        per_device,
        mesh=axes,
        in_specs=(
            P(("x", "zh"), None, ("y", "k", "zl")),
            P(("y", "k", "x", "zh"), "zl"),
            P(("y", "k", "x", "zh"), "zl"),
            P(("x", "zh"), ("y", "k"), "zl"),
        ),
        out_specs=(
            P(("x", "zh"), ("y", "k"), "zl"),
            P(("x", "zh"), None, ("y", "k", "zl")),
            P(("y", "k", "x", "zh"), "zl"),
        ),
        check_vma=False,
    )
```

```python
import jax
import jax.numpy as jnp
from jax import lax
from jax.experimental import pallas as pl
from jax.experimental.pallas import tpu as pltpu
from jax.sharding import Mesh, PartitionSpec as P

BLOCK = 128
BF = jnp.bfloat16
F32 = jnp.float32
VMEM_LIMIT = 56 * 1024 * 1024


def params():
    return pltpu.CompilerParams(vmem_limit_bytes=VMEM_LIMIT)


def cost(flops, moved):
    return pl.CostEstimate(flops=flops, bytes_accessed=moved, transcendentals=0)


def whole(shape):
    return pl.BlockSpec(shape, lambda *_: (0,) * len(shape))


SCALAR = pl.BlockSpec(memory_space=pltpu.SMEM)
ANY = pl.BlockSpec(memory_space=pl.ANY)


def ring(size, step):
    return [(i, (i + step) % size) for i in range(size)]


def dequantize_kernel(scales, quantized, top, bottom):
    for r, half in enumerate((top, bottom)):
        for c in range(scales.shape[1]):
            lanes = pl.ds(c * BLOCK, BLOCK)
            block = quantized[pl.ds(r * BLOCK, BLOCK), lanes].astype(F32)
            half[:, lanes] = (block * scales[r, c]).astype(BF)


def dequantize(scales, quantized):
    half = (BLOCK, quantized.shape[1])
    return pl.pallas_call(
        dequantize_kernel,
        out_shape=[jax.ShapeDtypeStruct(half, BF)] * 2,
        in_specs=[SCALAR, whole(quantized.shape)],
        out_specs=[whole(half)] * 2,
        compiler_params=params(),
        cost_estimate=cost(1, 1),
    )(scales, quantized)


def split_kernel(inputs, split):
    for at in range(8):
        split[at] = inputs[:, at % 2 * 256 : at % 2 * 256 + 256]


def split_units(inputs):
    shape = (8, 512, 256)
    return pl.pallas_call(
        split_kernel,
        out_shape=jax.ShapeDtypeStruct(shape, BF),
        in_specs=[whole(inputs.shape)],
        out_specs=whole(shape),
        compiler_params=params(),
        cost_estimate=cost(1, 1),
    )(inputs)


PRODUCT = cost(1, 1)


def stacked(refs):
    return jnp.concatenate([ref[...] for ref in refs], axis=0)


def halves(top, bottom, top_up, up, down, bottom_down):
    first, second = pl.ds(0, BLOCK), pl.ds(BLOCK, BLOCK)
    return (
        top, bottom, top_up, up.at[second],
        up.at[first], down.at[second], down.at[first], bottom_down,
    )


def forward_kernel(place, _, panel, *refs):
    weights, (own, other, left) = halves(*refs[:6]), refs[6:]
    x, k, zh = place[0], place[2], place[3]

    @pl.when(pl.program_id(0) == 0)
    def _():
        for at in range(8):
            m = lax.rem(x - at // 2 + 4, 4)
            s = lax.rem(at % 2 + zh, 2)
            lanes = pl.ds(pl.multiple_of(m * 256, 256), 256)
            for b in range(8):
                kk = lax.rem(k + b % 2, 2)
                row = kk * 512 + b // 2 * 128 + s * 64
                rows = pl.ds(pl.multiple_of(row, 64), 64)
                left[rows, lanes] = panel[at, b * 64 : b * 64 + 64, :]

    total = jnp.dot(left[...], stacked(weights), preferred_element_type=F32)
    own[...] = total[:512].astype(BF)
    other[...] = total[512:].astype(BF)


def forward(place, after, panel, weights):
    width = weights[0].shape[1]
    tile = width // 3
    return pl.pallas_call(
        forward_kernel,
        grid=(width // tile,),
        out_shape=[jax.ShapeDtypeStruct((512, width), BF)] * 2,
        in_specs=[SCALAR, ANY, whole(panel.shape)]
        + [pl.BlockSpec((w.shape[0], tile), lambda n: (0, n)) for w in weights],
        out_specs=[pl.BlockSpec((512, tile), lambda n: (0, n))] * 2,
        scratch_shapes=[pltpu.VMEM((1024, 1024), BF)],
        compiler_params=params(),
        cost_estimate=PRODUCT,
    )(place, after, panel, *weights)


def weight_grad_kernel(place, _, panel, near, *refs):
    far, outs, (left, right) = refs[:4], refs[4:9], refs[9:]
    x, y, k, zh = place[0], place[1], place[2], place[3]

    @pl.when(pl.program_id(0) == 0)
    def _():
        for at in range(8):
            m = lax.rem(x - at // 2 + 4, 4)
            s = lax.rem(at % 2 + zh, 2)
            rows = pl.ds(pl.multiple_of(m * 256, 256), 256)
            lanes = pl.ds(pl.multiple_of(s * 512, 512), 512)
            left[rows, lanes] = panel[at].T

    right[:512, :] = near[...]
    for e in range(4):
        for kk in range(2):
            block = lax.rem(y - e + 4, 4) * 2 + lax.rem(k + kk, 2)
            rows = pl.ds(pl.multiple_of(512 + block * 64, 64), 64)
            right[rows, :] = far[e][kk * 64 : kk * 64 + 64, :]
    total = jnp.dot(left[...], right[...], preferred_element_type=F32)
    at = 0
    for out in outs:
        out[...] = total[at : at + out.shape[0]].astype(BF)
        at += out.shape[0]


def weight_grad(place, after, panel, near, far):
    width = near.shape[1]
    tile = width // 3
    sizes = (256, 256, 128, 128, 256)
    return pl.pallas_call(
        weight_grad_kernel,
        grid=(width // tile,),
        out_shape=[jax.ShapeDtypeStruct((rows, width), BF) for rows in sizes],
        in_specs=[SCALAR, ANY, whole(panel.shape)]
        + [pl.BlockSpec((rows, tile), lambda n: (0, n)) for rows in (512, 128, 128, 128, 128)],
        out_specs=[pl.BlockSpec((rows, tile), lambda n: (0, n)) for rows in sizes],
        scratch_shapes=[pltpu.VMEM((1024, 1024), BF), pltpu.VMEM((1024, tile), BF)],
        compiler_params=params(),
        cost_estimate=PRODUCT,
    )(place, after, panel, near, *far)


def backward_kernel(place, near, *refs):
    far, weights, out = refs[:4], halves(*refs[4:10]), refs[10]
    x, y, k, zh = place[0], place[1], place[2], place[3]
    step = pl.program_id(0)
    rows = pl.ds(pl.multiple_of(step * 256, 256), 256)
    far = stacked(far)
    for m in range(4):
        at = lax.rem(x - m + 4, 4) * 2
        right = stacked(weights[2 * m : 2 * m + 2])
        total = lax.dot_general(
            near[...], right, (((1,), (1,)), ((), ())), preferred_element_type=F32
        )
        out[at + zh, rows, :] = total.astype(BF)
        total = lax.dot_general(
            far, right, (((1,), (1,)), ((), ())), preferred_element_type=F32
        ).astype(BF)
        for i in range(4):
            block = lax.rem(y - i + 4, 4) * 2 + lax.rem(k + step, 2)
            target = pl.ds(pl.multiple_of(block * 64, 64), 64)
            out[at + 1 - zh, target, :] = total[i * 64 : i * 64 + 64]


def backward(place, near, far, weights):
    width = near.shape[1]
    return pl.pallas_call(
        backward_kernel,
        grid=(2,),
        out_shape=jax.ShapeDtypeStruct((8, 512, 256), BF),
        in_specs=[SCALAR]
        + [pl.BlockSpec((rows, width), lambda n: (n, 0)) for rows in (256, 64, 64, 64, 64)]
        + [whole(w.shape) for w in weights],
        out_specs=whole((8, 512, 256)),
        compiler_params=params(),
        cost_estimate=PRODUCT,
    )(place, near, *far, *weights)


def summed(*refs):
    total = refs[0].astype(F32)
    for ref in refs[1:]:
        total = total + ref.astype(F32)
    return total.astype(BF)


def local(kernel, outs, after, *args):
    after = after if isinstance(after, tuple) else (after,)
    return pl.pallas_call(
        lambda *refs: kernel(*refs[len(after) :]),
        out_shape=[jax.ShapeDtypeStruct(shape, BF) for shape in outs],
        in_specs=[ANY] * len(after) + [whole(a.shape) for a in args],
        out_specs=[whole(shape) for shape in outs],
        compiler_params=params(),
        cost_estimate=cost(1, 1),
    )(*after, *args)


def follow(array, after):
    return pl.pallas_call(
        lambda *_: None,
        out_shape=jax.ShapeDtypeStruct(array.shape, array.dtype),
        in_specs=[ANY] * (1 + len(after)),
        out_specs=ANY,
        input_output_aliases={0: 0},
        cost_estimate=cost(1, 1),
    )(array, *after)


def relay_kernel(top, bottom, top_up, bottom_down, up, down):
    up[:BLOCK], up[BLOCK:] = top_up[...], bottom[...]
    down[:BLOCK], down[BLOCK:] = top[...], bottom_down[...]


def collect_kernel(mine, theirs, out):
    out[:64], out[64:] = mine[...], theirs[...]


def sum_kernel(*refs):
    refs[-1][...] = summed(*[ref[...] for ref in refs[:-1]])


def onward_kernel(up, down, from_below, from_above, up_out, down_out):
    half = from_below.shape[0]
    up_out[:half] = summed(up[:half], from_below[...])
    up_out[half:] = up[half:]
    down_out[:half] = down[:half]
    down_out[half:] = summed(down[half:], from_above[...])


def shift(array, axis, step):
    return lax.ppermute(array, axis, ring(lax.axis_size(axis), step))


def per_device(inputs, qweight, scales, grad_out):
    x, y, k, zh = (lax.axis_index(name) for name in ("x", "y", "k", "zh"))
    place = jnp.stack([x, y, k, zh]).astype(jnp.int32)
    F = qweight.shape[1]

    near = lax.all_gather(grad_out[0], ("y", "k"), axis=0, tiled=True)

    far = shift(grad_out[0], "zh", 1)
    top, bottom = dequantize(scales, qweight)
    top_up, bottom_down = shift(top, "x", 1), shift(bottom, "x", -1)
    split = follow(split_units(inputs[0]), (far, top_up, bottom_down))
    panel = lax.all_to_all(split, ("zl", "zh"), 0, 0, tiled=True)
    up, down = local(
        relay_kernel, [(256, F)] * 2, (), top, bottom, top_up, bottom_down
    )
    (far,) = local(collect_kernel, [(128, F)], up, far, shift(far, "k", 1))
    far = [far] + [shift(far, "y", e) for e in (1, 2, 3)]
    up, down = shift(up, "x", 1), shift(down, "x", -1)
    weights = (top, bottom, top_up, up, down, bottom_down)

    sums = backward(place, near, far, weights)
    own, other = forward(place, sums, panel, weights)
    other = shift(other, "k", 1)
    terms = weight_grad(place, own, panel, near, far)

    (both,) = local(sum_kernel, [(512, F)], terms[0], own, other)
    both = lax.psum_scatter(both, "y", scatter_dimension=0, tiled=True)
    projected = summed(both[:64], shift(both[64:], "zh", 1))

    sums = lax.all_to_all(sums, ("zl", "zh"), 0, 0, tiled=True)
    grad_inputs = jnp.concatenate(
        [summed(*[sums[zl * 2 + h] for zl in range(4)]) for h in range(2)], axis=1
    )

    here, down, top, bottom, up = terms
    top, bottom = shift(top, "x", 1), shift(bottom, "x", -1)
    up, down = local(onward_kernel, [(256, F)] * 2, (), up, down, top, bottom)
    up, down = shift(up, "x", 1), shift(down, "x", -1)
    (grad_weight,) = local(sum_kernel, [(256, F)], grad_inputs, here, up, down)

    return projected[None], grad_inputs[None], grad_weight


def solution(mesh):
    axes = Mesh(mesh.devices.reshape(4, 2, 4, 4, 2), ("y", "k", "zl", "x", "zh"))
    return jax.shard_map(
        per_device,
        mesh=axes,
        in_specs=(
            P(("x", "zh"), None, ("y", "k", "zl")),
            P(("y", "k", "x", "zh"), "zl"),
            P(("y", "k", "x", "zh"), "zl"),
            P(("x", "zh"), ("y", "k"), "zl"),
        ),
        out_specs=(
            P(("x", "zh"), ("y", "k"), "zl"),
            P(("x", "zh"), None, ("y", "k", "zl")),
            P(("y", "k", "x", "zh"), "zl"),
        ),
        check_vma=False,
    )
```

```python
import jax
import jax.numpy as jnp
from jax import lax
from jax.experimental import pallas as pl
from jax.experimental.pallas import tpu as pltpu
from jax.sharding import Mesh, PartitionSpec as P

BLOCK = 128
BF = jnp.bfloat16
F32 = jnp.float32
VMEM_LIMIT = 56 * 1024 * 1024


def params():
    return pltpu.CompilerParams(vmem_limit_bytes=VMEM_LIMIT)


def cost(flops, moved):
    return pl.CostEstimate(flops=flops, bytes_accessed=moved, transcendentals=0)


def whole(shape):
    return pl.BlockSpec(shape, lambda *_: (0,) * len(shape))


SCALAR = pl.BlockSpec(memory_space=pltpu.SMEM)
ANY = pl.BlockSpec(memory_space=pl.ANY)


def ring(size, step):
    return [(i, (i + step) % size) for i in range(size)]


def dequantize_kernel(scales, quantized, top, bottom):
    for r, half in enumerate((top, bottom)):
        for c in range(scales.shape[1]):
            lanes = pl.ds(c * BLOCK, BLOCK)
            block = quantized[pl.ds(r * BLOCK, BLOCK), lanes].astype(F32)
            half[:, lanes] = (block * scales[r, c]).astype(BF)


def dequantize(scales, quantized):
    half = (BLOCK, quantized.shape[1])
    return pl.pallas_call(
        dequantize_kernel,
        out_shape=[jax.ShapeDtypeStruct(half, BF)] * 2,
        in_specs=[SCALAR, whole(quantized.shape)],
        out_specs=[whole(half)] * 2,
        compiler_params=params(),
        cost_estimate=cost(1, 1),
    )(scales, quantized)


def split_kernel(inputs, split):
    for at in range(8):
        split[at] = inputs[:, at % 2 * 256 : at % 2 * 256 + 256]


def split_units(inputs):
    shape = (8, 512, 256)
    return pl.pallas_call(
        split_kernel,
        out_shape=jax.ShapeDtypeStruct(shape, BF),
        in_specs=[whole(inputs.shape)],
        out_specs=whole(shape),
        compiler_params=params(),
        cost_estimate=cost(1, 1),
    )(inputs)


PRODUCT = cost(1, 1)


def stacked(refs):
    return jnp.concatenate([ref[...] for ref in refs], axis=0)


def halves(top, bottom, top_up, up, down, bottom_down):
    first, second = pl.ds(0, BLOCK), pl.ds(BLOCK, BLOCK)
    return (
        top, bottom, top_up, up.at[second],
        up.at[first], down.at[second], down.at[first], bottom_down,
    )


def forward_kernel(place, _, panel, *refs):
    weights, (out, left) = halves(*refs[:6]), refs[6:]
    x, zh = place[0], place[1]

    @pl.when(pl.program_id(0) == 0)
    def _():
        for at in range(8):
            m = lax.rem(x - at // 2 + 4, 4)
            s = lax.rem(at % 2 + zh, 2)
            lanes = pl.ds(pl.multiple_of(m * 256, 256), 256)
            for b in range(8):
                rows = pl.ds(pl.multiple_of(b * 128 + s * 64, 64), 64)
                left[rows, lanes] = panel[at, b * 64 : b * 64 + 64, :]

    total = jnp.dot(left[...], stacked(weights), preferred_element_type=F32)
    out[...] = total.astype(BF)


def forward(place, after, panel, weights):
    width = weights[0].shape[1]
    tile = width // 3
    return pl.pallas_call(
        forward_kernel,
        grid=(width // tile,),
        out_shape=jax.ShapeDtypeStruct((1024, width), BF),
        in_specs=[SCALAR, ANY, whole(panel.shape)]
        + [pl.BlockSpec((w.shape[0], tile), lambda n: (0, n)) for w in weights],
        out_specs=pl.BlockSpec((1024, tile), lambda n: (0, n)),
        scratch_shapes=[pltpu.VMEM((1024, 1024), BF)],
        compiler_params=params(),
        cost_estimate=PRODUCT,
    )(place, after, panel, *weights)


def weight_grad_kernel(place, _, panel, grad, *refs):
    outs, left = refs[:5], refs[5]

    @pl.when(pl.program_id(0) == 0)
    def _():
        for at in range(8):
            m = lax.rem(place[0] - at // 2 + 4, 4)
            s = lax.rem(at % 2 + place[1], 2)
            rows = pl.ds(pl.multiple_of(m * 256, 256), 256)
            lanes = pl.ds(pl.multiple_of(s * 512, 512), 512)
            left[rows, lanes] = panel[at].T

    total = jnp.dot(left[...], grad[...], preferred_element_type=F32)
    at = 0
    for out in outs:
        out[...] = total[at : at + out.shape[0]].astype(BF)
        at += out.shape[0]


def weight_grad(place, after, panel, grad):
    width = grad.shape[1]
    tile = width // 3
    sizes = (256, 256, 128, 128, 256)
    return pl.pallas_call(
        weight_grad_kernel,
        grid=(width // tile,),
        out_shape=[jax.ShapeDtypeStruct((rows, width), BF) for rows in sizes],
        in_specs=[
            SCALAR,
            ANY,
            whole(panel.shape),
            pl.BlockSpec((1024, tile), lambda n: (0, n)),
        ],
        out_specs=[pl.BlockSpec((rows, tile), lambda n: (0, n)) for rows in sizes],
        scratch_shapes=[pltpu.VMEM((1024, 1024), BF)],
        compiler_params=params(),
        cost_estimate=PRODUCT,
    )(place, after, panel, grad)


def backward_kernel(place, *refs):
    grads, weights, out = refs[:2], halves(*refs[2:8]), refs[8]
    rows = pl.ds(pl.multiple_of(pl.program_id(0) * 256, 256), 256)
    for m in range(4):
        at = lax.rem(place[0] - m + 4, 4) * 2
        right = stacked(weights[2 * m : 2 * m + 2])
        for s, grad in enumerate(grads):
            total = lax.dot_general(
                grad[...], right, (((1,), (1,)), ((), ())), preferred_element_type=F32
            )
            out[at + lax.rem(s + place[1], 2), rows, :] = total.astype(BF)


def backward(place, grad, weights):
    width = grad.shape[1]
    return pl.pallas_call(
        backward_kernel,
        grid=(2,),
        out_shape=jax.ShapeDtypeStruct((8, 512, 256), BF),
        in_specs=[
            SCALAR,
            pl.BlockSpec((256, width), lambda n: (n, 0)),
            pl.BlockSpec((256, width), lambda n: (n + 2, 0)),
        ]
        + [whole(w.shape) for w in weights],
        out_specs=whole((8, 512, 256)),
        compiler_params=params(),
        cost_estimate=PRODUCT,
    )(place, grad, grad, *weights)


def summed(*refs):
    total = refs[0].astype(F32)
    for ref in refs[1:]:
        total = total + ref.astype(F32)
    return total.astype(BF)


def local(kernel, outs, after, *args):
    after = after if isinstance(after, tuple) else (after,)
    return pl.pallas_call(
        lambda *refs: kernel(*refs[len(after) :]),
        out_shape=[jax.ShapeDtypeStruct(shape, BF) for shape in outs],
        in_specs=[ANY] * len(after) + [whole(a.shape) for a in args],
        out_specs=[whole(shape) for shape in outs],
        compiler_params=params(),
        cost_estimate=cost(1, 1),
    )(*after, *args)


def follow(array, after):
    return pl.pallas_call(
        lambda *_: None,
        out_shape=jax.ShapeDtypeStruct(array.shape, array.dtype),
        in_specs=[ANY] * (1 + len(after)),
        out_specs=ANY,
        input_output_aliases={0: 0},
        cost_estimate=cost(1, 1),
    )(array, *after)


def relay_kernel(top, bottom, top_up, bottom_down, mine, theirs, up, down, both):
    up[:BLOCK], up[BLOCK:] = top_up[...], bottom[...]
    down[:BLOCK], down[BLOCK:] = top[...], bottom_down[...]
    both[0], both[1] = mine[...], theirs[...]


def sum_kernel(*refs):
    refs[-1][...] = summed(*[ref[...] for ref in refs[:-1]])


def gather_kernel(sums, out):
    for h in range(2):
        lanes = pl.ds(h * 256, 256)
        out[:, lanes] = summed(*[sums[zl * 2 + h] for zl in range(4)])


def onward_kernel(up, down, from_below, from_above, up_out, down_out):
    half = from_below.shape[0]
    up_out[:half] = summed(up[:half], from_below[...])
    up_out[half:] = up[half:]
    down_out[:half] = down[:half]
    down_out[half:] = summed(down[half:], from_above[...])


def shift(array, axis, step):
    return lax.ppermute(array, axis, ring(lax.axis_size(axis), step))


def per_device(inputs, qweight, scales, grad_out):
    x, zh = lax.axis_index("x"), lax.axis_index("zh")
    place = jnp.stack([x, zh]).astype(jnp.int32)
    F = qweight.shape[1]

    top, bottom = dequantize(scales, qweight)
    top_up, bottom_down = shift(top, "x", 1), shift(bottom, "x", -1)
    up, down, both = local(
        relay_kernel,
        [(256, F), (256, F), (2, 64, F)],
        (),
        *(top, bottom, top_up, bottom_down),
        *(grad_out[0], shift(grad_out[0], "zh", 1)),
    )
    grad = lax.all_gather(both, ("y", "k"), axis=1, tiled=True).reshape(1024, F)

    split = follow(split_units(inputs[0]), (up,))
    panel = lax.all_to_all(split, ("zl", "zh"), 0, 0, tiled=True)

    up, down = shift(up, "x", 1), shift(down, "x", -1)
    weights = (top, bottom, top_up, up, down, bottom_down)

    sums = backward(place, grad, weights)
    product = forward(place, sums, panel, weights)
    terms = weight_grad(place, product, panel, grad)

    product = lax.psum_scatter(product, ("y", "k"), scatter_dimension=0, tiled=True)
    projected = summed(product[:64], shift(product[64:], "zh", 1))

    sums = lax.all_to_all(sums, ("zl", "zh"), 0, 0, tiled=True)
    (grad_inputs,) = local(gather_kernel, [(512, 512)], (), sums)

    here, down, top, bottom, up = terms
    top, bottom = shift(top, "x", 1), shift(bottom, "x", -1)
    up, down = local(onward_kernel, [(256, F)] * 2, (), up, down, top, bottom)
    up, down = shift(up, "x", 1), shift(down, "x", -1)
    (grad_weight,) = local(sum_kernel, [(256, F)], (), here, up, down)

    return projected[None], grad_inputs[None], grad_weight


def solution(mesh):
    axes = Mesh(mesh.devices.reshape(4, 2, 4, 4, 2), ("y", "k", "zl", "x", "zh"))
    return jax.shard_map(
        per_device,
        mesh=axes,
        in_specs=(
            P(("x", "zh"), None, ("y", "k", "zl")),
            P(("y", "k", "x", "zh"), "zl"),
            P(("y", "k", "x", "zh"), "zl"),
            P(("x", "zh"), ("y", "k"), "zl"),
        ),
        out_specs=(
            P(("x", "zh"), ("y", "k"), "zl"),
            P(("x", "zh"), None, ("y", "k", "zl")),
            P(("y", "k", "x", "zh"), "zl"),
        ),
        check_vma=False,
    )
```

```python
import jax
import jax.numpy as jnp
from jax import lax
from jax.experimental import pallas as pl
from jax.experimental.pallas import tpu as pltpu
from jax.sharding import Mesh, PartitionSpec as P

BLOCK = 128
BF = jnp.bfloat16
F32 = jnp.float32
VMEM_LIMIT = 62 * 1024 * 1024


def params():
    return pltpu.CompilerParams(vmem_limit_bytes=VMEM_LIMIT)


def cost(flops, moved):
    return pl.CostEstimate(flops=flops, bytes_accessed=moved, transcendentals=0)


def whole(shape):
    return pl.BlockSpec(shape, lambda *_: (0,) * len(shape))


SCALAR = pl.BlockSpec(memory_space=pltpu.SMEM)
ANY = pl.BlockSpec(memory_space=pl.ANY)


def ring(size, step):
    return [(i, (i + step) % size) for i in range(size)]


def dequantize_kernel(scales, quantized, top, bottom):
    for r, half in enumerate((top, bottom)):
        for c in range(scales.shape[1]):
            lanes = pl.ds(c * BLOCK, BLOCK)
            block = quantized[pl.ds(r * BLOCK, BLOCK), lanes].astype(F32)
            half[:, lanes] = (block * scales[r, c]).astype(BF)


def dequantize(scales, quantized):
    half = (BLOCK, quantized.shape[1])
    return pl.pallas_call(
        dequantize_kernel,
        out_shape=[jax.ShapeDtypeStruct(half, BF)] * 2,
        in_specs=[SCALAR, whole(quantized.shape)],
        out_specs=[whole(half)] * 2,
        compiler_params=params(),
        cost_estimate=cost(1, 1),
    )(scales, quantized)


def split_kernel(inputs, split):
    for at in range(8):
        split[at] = inputs[:, at % 2 * 256 : at % 2 * 256 + 256]


def split_units(inputs):
    shape = (8, 512, 256)
    return pl.pallas_call(
        split_kernel,
        out_shape=jax.ShapeDtypeStruct(shape, BF),
        in_specs=[whole(inputs.shape)],
        out_specs=whole(shape),
        compiler_params=params(),
        cost_estimate=cost(1, 1),
    )(inputs)


PRODUCT = cost(1, 1)


def stacked(refs):
    return jnp.concatenate([ref[...] for ref in refs], axis=0)


def halves(top, bottom, top_up, up, down, bottom_down):
    first, second = pl.ds(0, BLOCK), pl.ds(BLOCK, BLOCK)
    return (
        top, bottom, top_up, up.at[second],
        up.at[first], down.at[second], down.at[first], bottom_down,
    )


def forward_kernel(place, _, panel, *refs):
    weights, (out, left) = halves(*refs[:6]), refs[6:]
    x, zh = place[0], place[1]

    @pl.when(pl.program_id(0) == 0)
    def _():
        for at in range(8):
            m = lax.rem(x - at // 2 + 4, 4)
            s = lax.rem(at % 2 + zh, 2)
            lanes = pl.ds(pl.multiple_of(m * 256, 256), 256)
            for b in range(8):
                rows = pl.ds(pl.multiple_of(b * 128 + s * 64, 64), 64)
                left[rows, lanes] = panel[at, b * 64 : b * 64 + 64, :]

    total = jnp.dot(left[...], stacked(weights), preferred_element_type=F32)
    out[...] = total.astype(BF)


def forward(place, after, panel, weights):
    width = weights[0].shape[1]
    tile = width // 3
    return pl.pallas_call(
        forward_kernel,
        grid=(width // tile,),
        out_shape=jax.ShapeDtypeStruct((1024, width), BF),
        in_specs=[SCALAR, ANY, whole(panel.shape)]
        + [pl.BlockSpec((w.shape[0], tile), lambda n: (0, n)) for w in weights],
        out_specs=pl.BlockSpec((1024, tile), lambda n: (0, n)),
        scratch_shapes=[pltpu.VMEM((1024, 1024), BF)],
        compiler_params=params(),
        cost_estimate=PRODUCT,
    )(place, after, panel, *weights)


def weight_grad_kernel(place, _, panel, near, far, *refs):
    outs, left = refs[:5], refs[5]

    @pl.when(pl.program_id(0) == 0)
    def _():
        for at in range(8):
            m = lax.rem(place[0] - at // 2 + 4, 4)
            s = lax.rem(at % 2 + place[1], 2)
            rows = pl.ds(pl.multiple_of(m * 256, 256), 256)
            lanes = pl.ds(pl.multiple_of(s * 512, 512), 512)
            left[rows, lanes] = panel[at].T

    total = jnp.dot(left[...], stacked((near, far)), preferred_element_type=F32)
    at = 0
    for out in outs:
        out[...] = total[at : at + out.shape[0]].astype(BF)
        at += out.shape[0]


def weight_grad(place, after, panel, near, far):
    width = near.shape[1]
    tile = width // 3
    sizes = (256, 256, 128, 128, 256)
    return pl.pallas_call(
        weight_grad_kernel,
        grid=(width // tile,),
        out_shape=[jax.ShapeDtypeStruct((rows, width), BF) for rows in sizes],
        in_specs=[
            SCALAR,
            ANY,
            whole(panel.shape),
            pl.BlockSpec((512, tile), lambda n: (0, n)),
            pl.BlockSpec((512, tile), lambda n: (0, n)),
        ],
        out_specs=[pl.BlockSpec((rows, tile), lambda n: (0, n)) for rows in sizes],
        scratch_shapes=[pltpu.VMEM((1024, 1024), BF)],
        compiler_params=params(),
        cost_estimate=PRODUCT,
    )(place, after, panel, near, far)


def backward_kernel(place, *refs):
    grads, weights, out = refs[:2], halves(*refs[2:8]), refs[8]
    rows = pl.ds(pl.multiple_of(pl.program_id(0) * 256, 256), 256)
    for m in range(4):
        at = lax.rem(place[0] - m + 4, 4) * 2
        right = stacked(weights[2 * m : 2 * m + 2])
        for s, grad in enumerate(grads):
            total = lax.dot_general(
                grad[...], right, (((1,), (1,)), ((), ())), preferred_element_type=F32
            )
            out[at + lax.rem(s + place[1], 2), rows, :] = total.astype(BF)


def backward(place, near, far, weights):
    width = near.shape[1]
    return pl.pallas_call(
        backward_kernel,
        grid=(2,),
        out_shape=jax.ShapeDtypeStruct((8, 512, 256), BF),
        in_specs=[
            SCALAR,
            pl.BlockSpec((256, width), lambda n: (n, 0)),
            pl.BlockSpec((256, width), lambda n: (n, 0)),
        ]
        + [whole(w.shape) for w in weights],
        out_specs=whole((8, 512, 256)),
        compiler_params=params(),
        cost_estimate=PRODUCT,
    )(place, near, far, *weights)


def summed(*refs):
    total = refs[0].astype(F32)
    for ref in refs[1:]:
        total = total + ref.astype(F32)
    return total.astype(BF)


def local(kernel, outs, after, *args):
    after = after if isinstance(after, tuple) else (after,)
    return pl.pallas_call(
        lambda *refs: kernel(*refs[len(after) :]),
        out_shape=[jax.ShapeDtypeStruct(shape, BF) for shape in outs],
        in_specs=[ANY] * len(after) + [whole(a.shape) for a in args],
        out_specs=[whole(shape) for shape in outs],
        compiler_params=params(),
        cost_estimate=cost(1, 1),
    )(*after, *args)


def relay_kernel(top, bottom, top_up, bottom_down, far, up, down, passed):
    up[:BLOCK], up[BLOCK:] = top_up[...], bottom[...]
    down[:BLOCK], down[BLOCK:] = top[...], bottom_down[...]
    passed[...] = far[...]


def sum_kernel(*refs):
    refs[-1][...] = summed(*[ref[...] for ref in refs[:-1]])


def end_kernel(mine, theirs, out):
    out[...] = summed(mine[:64], theirs[...])


def gather_kernel(sums, out):
    for h in range(2):
        lanes = pl.ds(h * 256, 256)
        out[:, lanes] = summed(*[sums[zl * 2 + h] for zl in range(4)])


def onward_kernel(up, down, from_below, from_above, up_out, down_out):
    half = from_below.shape[0]
    up_out[:half] = summed(up[:half], from_below[...])
    up_out[half:] = up[half:]
    down_out[:half] = down[:half]
    down_out[half:] = summed(down[half:], from_above[...])


def shift(array, axis, step):
    return lax.ppermute(array, axis, ring(lax.axis_size(axis), step))


def per_device(inputs, qweight, scales, grad_out):
    x, zh = lax.axis_index("x"), lax.axis_index("zh")
    place = jnp.stack([x, zh]).astype(jnp.int32)
    F = qweight.shape[1]

    near = lax.all_gather(grad_out[0], ("y", "k"), axis=0, tiled=True)
    split = split_units(inputs[0])
    panel = lax.all_to_all(split, ("zl", "zh"), 0, 0, tiled=True)

    top, bottom = dequantize(scales, qweight)
    top_up, bottom_down = shift(top, "x", 1), shift(bottom, "x", -1)
    far = shift(grad_out[0], "zh", 1)
    up, down, far = local(
        relay_kernel,
        [(256, F), (256, F), (64, F)],
        split,
        *(top, bottom, top_up, bottom_down, far),
    )
    far = lax.all_gather(far, ("y", "k"), axis=0, tiled=True)
    up, down = shift(up, "x", 1), shift(down, "x", -1)
    weights = (top, bottom, top_up, up, down, bottom_down)

    sums = backward(place, near, far, weights)
    product = forward(place, sums, panel, weights)
    terms = weight_grad(place, product, panel, near, far)

    product = lax.psum_scatter(product, ("y", "k"), scatter_dimension=0, tiled=True)
    (projected,) = local(
        end_kernel, [(64, F)], (), product, shift(product[64:], "zh", 1)
    )

    sums = lax.all_to_all(sums, ("zl", "zh"), 0, 0, tiled=True)
    (grad_inputs,) = local(gather_kernel, [(512, 512)], (), sums)

    here, down, top, bottom, up = terms
    top, bottom = shift(top, "x", 1), shift(bottom, "x", -1)
    up, down = local(onward_kernel, [(256, F)] * 2, (), up, down, top, bottom)
    up, down = shift(up, "x", 1), shift(down, "x", -1)
    (grad_weight,) = local(sum_kernel, [(256, F)], (grad_inputs, projected), here, up, down)

    return projected[None], grad_inputs[None], grad_weight


def solution(mesh):
    axes = Mesh(mesh.devices.reshape(4, 2, 4, 4, 2), ("y", "k", "zl", "x", "zh"))
    return jax.shard_map(
        per_device,
        mesh=axes,
        in_specs=(
            P(("x", "zh"), None, ("y", "k", "zl")),
            P(("y", "k", "x", "zh"), "zl"),
            P(("y", "k", "x", "zh"), "zl"),
            P(("x", "zh"), ("y", "k"), "zl"),
        ),
        out_specs=(
            P(("x", "zh"), ("y", "k"), "zl"),
            P(("x", "zh"), None, ("y", "k", "zl")),
            P(("y", "k", "x", "zh"), "zl"),
        ),
        check_vma=False,
    )
```

```python
import jax
import jax.numpy as jnp
from jax import lax
from jax.experimental import pallas as pl
from jax.experimental.pallas import tpu as pltpu
from jax.sharding import Mesh, PartitionSpec as P

BLOCK = 128
BF = jnp.bfloat16
F32 = jnp.float32
VMEM_LIMIT = 62 * 1024 * 1024


def params():
    return pltpu.CompilerParams(vmem_limit_bytes=VMEM_LIMIT)


def cost(flops, moved):
    return pl.CostEstimate(flops=flops, bytes_accessed=moved, transcendentals=0)


def whole(shape):
    return pl.BlockSpec(shape, lambda *_: (0,) * len(shape))


SCALAR = pl.BlockSpec(memory_space=pltpu.SMEM)
ANY = pl.BlockSpec(memory_space=pl.ANY)


def ring(size, step):
    return [(i, (i + step) % size) for i in range(size)]


def dequantize_kernel(scales, quantized, top, bottom, *quarters):
    for r, half in enumerate((top, bottom)):
        for c in range(scales.shape[1]):
            lanes = pl.ds(c * BLOCK, BLOCK)
            block = quantized[pl.ds(r * BLOCK, BLOCK), lanes].astype(F32)
            block = (block * scales[r, c]).astype(BF)
            half[:, lanes] = block
            quarters[2 * r][:, lanes] = block[:64]
            quarters[2 * r + 1][:, lanes] = block[64:]


def dequantize(scales, quantized):
    width = quantized.shape[1]
    shapes = [(BLOCK, width)] * 2 + [(64, width)] * 4
    return pl.pallas_call(
        dequantize_kernel,
        out_shape=[jax.ShapeDtypeStruct(shape, BF) for shape in shapes],
        in_specs=[SCALAR, whole(quantized.shape)],
        out_specs=[whole(shape) for shape in shapes],
        compiler_params=params(),
        cost_estimate=cost(1, 1),
    )(scales, quantized)


def split_kernel(inputs, split):
    for at in range(8):
        split[at] = inputs[:, at % 2 * 256 : at % 2 * 256 + 256]


def split_units(inputs):
    shape = (8, 512, 256)
    return pl.pallas_call(
        split_kernel,
        out_shape=jax.ShapeDtypeStruct(shape, BF),
        in_specs=[whole(inputs.shape)],
        out_specs=whole(shape),
        compiler_params=params(),
        cost_estimate=cost(1, 1),
    )(inputs)


PRODUCT = cost(1, 1)


def stacked(refs):
    return jnp.concatenate([ref[...] for ref in refs], axis=0)


def halves(top, bottom, top_up, up, down, bottom_down):
    first, second = pl.ds(0, BLOCK), pl.ds(BLOCK, BLOCK)
    return (
        top, bottom, top_up, up.at[second],
        up.at[first], down.at[second], down.at[first], bottom_down,
    )


def forward_kernel(place, _, panel, *refs):
    weights, (out, left) = halves(*refs[:6]), refs[6:]
    x, zh = place[0], place[1]

    @pl.when(pl.program_id(0) == 0)
    def _():
        for at in range(8):
            m = lax.rem(x - at // 2 + 4, 4)
            s = lax.rem(at % 2 + zh, 2)
            lanes = pl.ds(pl.multiple_of(m * 256, 256), 256)
            for b in range(8):
                rows = pl.ds(pl.multiple_of(b * 128 + s * 64, 64), 64)
                left[rows, lanes] = panel[at, b * 64 : b * 64 + 64, :]

    total = jnp.dot(left[...], stacked(weights), preferred_element_type=F32)
    out[...] = total.astype(BF)


def forward(place, after, panel, weights):
    width = weights[0].shape[1]
    tile = width // 3
    return pl.pallas_call(
        forward_kernel,
        grid=(width // tile,),
        out_shape=jax.ShapeDtypeStruct((1024, width), BF),
        in_specs=[SCALAR, ANY, whole(panel.shape)]
        + [pl.BlockSpec((w.shape[0], tile), lambda n: (0, n)) for w in weights],
        out_specs=pl.BlockSpec((1024, tile), lambda n: (0, n)),
        scratch_shapes=[pltpu.VMEM((1024, 1024), BF)],
        compiler_params=params(),
        cost_estimate=PRODUCT,
    )(place, after, panel, *weights)


def weight_grad_kernel(place, _, panel, grad, *refs):
    outs, left = refs[:5], refs[5]

    @pl.when(pl.program_id(0) == 0)
    def _():
        for at in range(8):
            m = lax.rem(place[0] - at // 2 + 4, 4)
            rows = pl.ds(pl.multiple_of(m * 256, 256), 256)
            left[rows, pl.ds(at % 2 * 512, 512)] = panel[at].T

    total = jnp.dot(left[...], grad[...], preferred_element_type=F32)
    at = 0
    for out in outs:
        out[...] = total[at : at + out.shape[0]].astype(BF)
        at += out.shape[0]


def weight_grad(place, after, panel, grad):
    width = grad.shape[1]
    tile = width // 3
    sizes = (256, 256, 128, 128, 256)
    return pl.pallas_call(
        weight_grad_kernel,
        grid=(width // tile,),
        out_shape=[jax.ShapeDtypeStruct((rows, width), BF) for rows in sizes],
        in_specs=[
            SCALAR,
            ANY,
            whole(panel.shape),
            pl.BlockSpec((1024, tile), lambda n: (0, n)),
        ],
        out_specs=[pl.BlockSpec((rows, tile), lambda n: (0, n)) for rows in sizes],
        scratch_shapes=[pltpu.VMEM((1024, 1024), BF)],
        compiler_params=params(),
        cost_estimate=PRODUCT,
    )(place, after, panel, grad)


def backward_kernel(place, *refs):
    grads, weights, out = refs[:2], halves(*refs[2:8]), refs[8]
    rows = pl.ds(pl.multiple_of(pl.program_id(0) * 256, 256), 256)
    for m in range(4):
        at = lax.rem(place[0] - m + 4, 4) * 2
        right = stacked(weights[2 * m : 2 * m + 2])
        for h, grad in enumerate(grads):
            total = lax.dot_general(
                grad[...], right, (((1,), (1,)), ((), ())), preferred_element_type=F32
            )
            out[at + h, rows, :] = total.astype(BF)


def backward(place, grad, weights):
    width = grad.shape[1]
    return pl.pallas_call(
        backward_kernel,
        grid=(2,),
        out_shape=jax.ShapeDtypeStruct((8, 512, 256), BF),
        in_specs=[
            SCALAR,
            pl.BlockSpec((256, width), lambda n: (n, 0)),
            pl.BlockSpec((256, width), lambda n: (n + 2, 0)),
        ]
        + [whole(w.shape) for w in weights],
        out_specs=whole((8, 512, 256)),
        compiler_params=params(),
        cost_estimate=PRODUCT,
    )(place, grad, grad, *weights)


def summed(*refs):
    total = refs[0].astype(F32)
    for ref in refs[1:]:
        total = total + ref.astype(F32)
    return total.astype(BF)


def local(kernel, outs, after, *args):
    after = after if isinstance(after, tuple) else (after,)
    return pl.pallas_call(
        lambda *refs: kernel(*refs[len(after) :]),
        out_shape=[jax.ShapeDtypeStruct(shape, BF) for shape in outs],
        in_specs=[ANY] * len(after) + [whole(a.shape) for a in args],
        out_specs=[whole(shape) for shape in outs],
        compiler_params=params(),
        cost_estimate=cost(1, 1),
    )(*after, *args)


def twice_kernel(source, out):
    out[0], out[1] = source[...], source[...]


def pass_kernel(source, out):
    out[...] = source[...]


def relay_kernel(top, bottom, *refs):
    (top_up, bottom_down), (up, down, first, last) = (refs[:2], refs[2:4]), refs[4:]
    for i in range(2):
        rows = pl.ds(i * 64, 64)
        up[rows, :] = first[rows, :] = top_up[i][...]
        down[pl.ds(BLOCK + i * 64, 64), :] = last[rows, :] = bottom_down[i][...]
    up[BLOCK:], down[:BLOCK] = bottom[...], top[...]


def sum_kernel(*refs):
    refs[-1][...] = summed(*[ref[...] for ref in refs[:-1]])


def end_kernel(mine, theirs, out):
    out[...] = summed(mine[:64], theirs[...])


def gather_kernel(sums, out):
    for h in range(2):
        lanes = pl.ds(h * 256, 256)
        out[:, lanes] = summed(*[sums[zl * 2 + h] for zl in range(4)])


def onward_kernel(up, down, from_below, from_above, up_out, down_out):
    half = from_below.shape[0]
    up_out[:half] = summed(up[:half], from_below[...])
    up_out[half:] = up[half:]
    down_out[:half] = down[:half]
    down_out[half:] = summed(down[half:], from_above[...])


def shift(array, axis, step):
    return lax.ppermute(array, axis, ring(lax.axis_size(axis), step))


def per_device(inputs, qweight, scales, grad_out):
    x, zh = lax.axis_index("x"), lax.axis_index("zh")
    place = jnp.stack([x, zh]).astype(jnp.int32)
    F = qweight.shape[1]

    (grad,) = local(twice_kernel, [(2, 64, F)], (), grad_out[0])
    grad = lax.all_to_all(grad, "zh", 0, 0, tiled=True)
    top, bottom, *quarters = dequantize(scales, qweight)
    came = [shift(quarter, "x", 1) for quarter in quarters[:2]]
    came += [shift(quarter, "x", -1) for quarter in quarters[2:]]
    split = split_units(inputs[0])
    (grad,) = local(pass_kernel, [(2, 64, F)], (split, *came), grad)
    grad = lax.all_gather(grad, ("y", "k"), axis=1, tiled=True).reshape(1024, F)
    panel = lax.all_to_all(split, ("zl", "zh"), 0, 0, tiled=True)

    shapes = [(256, F), (256, F), (BLOCK, F), (BLOCK, F)]
    up, down, top_up, bottom_down = local(relay_kernel, shapes, (), top, bottom, *came)
    up, down = shift(up, "x", 1), shift(down, "x", -1)
    weights = (top, bottom, top_up, up, down, bottom_down)

    sums = backward(place, grad, weights)
    product = forward(place, sums, panel, weights)
    terms = weight_grad(place, product, panel, grad)

    product = lax.psum_scatter(product, ("y", "k"), scatter_dimension=0, tiled=True)
    (projected,) = local(
        end_kernel, [(64, F)], (), product, shift(product[64:], "zh", 1)
    )

    sums = lax.all_to_all(sums, ("zl", "zh"), 0, 0, tiled=True)
    (grad_inputs,) = local(gather_kernel, [(512, 512)], (), sums)

    here, down, top, bottom, up = terms
    top, bottom = shift(top, "x", 1), shift(bottom, "x", -1)
    up, down = local(onward_kernel, [(256, F)] * 2, (), up, down, top, bottom)
    up, down = shift(up, "x", 1), shift(down, "x", -1)
    (grad_weight,) = local(sum_kernel, [(256, F)], (grad_inputs, projected), here, up, down)

    return projected[None], grad_inputs[None], grad_weight


def solution(mesh):
    axes = Mesh(mesh.devices.reshape(4, 2, 4, 4, 2), ("y", "k", "zl", "x", "zh"))
    return jax.shard_map(
        per_device,
        mesh=axes,
        in_specs=(
            P(("x", "zh"), None, ("y", "k", "zl")),
            P(("y", "k", "x", "zh"), "zl"),
            P(("y", "k", "x", "zh"), "zl"),
            P(("x", "zh"), ("y", "k"), "zl"),
        ),
        out_specs=(
            P(("x", "zh"), ("y", "k"), "zl"),
            P(("x", "zh"), None, ("y", "k", "zl")),
            P(("y", "k", "x", "zh"), "zl"),
        ),
        check_vma=False,
    )
```

```python
import functools

import jax
import jax.numpy as jnp
from jax import lax
from jax.experimental import pallas as pl
from jax.experimental.pallas import tpu as pltpu
from jax.sharding import Mesh, PartitionSpec as P

BLOCK = 128
BF = jnp.bfloat16
F32 = jnp.float32
VMEM_LIMIT = 62 * 1024 * 1024


def params():
    return pltpu.CompilerParams(vmem_limit_bytes=VMEM_LIMIT)


def cost(flops, moved):
    return pl.CostEstimate(flops=flops, bytes_accessed=moved, transcendentals=0)


def whole(shape):
    return pl.BlockSpec(shape, lambda *_: (0,) * len(shape))


SCALAR = pl.BlockSpec(memory_space=pltpu.SMEM)
ANY = pl.BlockSpec(memory_space=pl.ANY)


def ring(size, step):
    return [(i, (i + step) % size) for i in range(size)]


def dequantize_kernel(scales, quantized, top, bottom):
    for r, half in enumerate((top, bottom)):
        for c in range(scales.shape[1]):
            lanes = pl.ds(c * BLOCK, BLOCK)
            block = quantized[pl.ds(r * BLOCK, BLOCK), lanes].astype(F32)
            half[:, lanes] = (block * scales[r, c]).astype(BF)


def dequantize(scales, quantized):
    half = (BLOCK, quantized.shape[1])
    return pl.pallas_call(
        dequantize_kernel,
        out_shape=[jax.ShapeDtypeStruct(half, BF)] * 2,
        in_specs=[SCALAR, whole(quantized.shape)],
        out_specs=[whole(half)] * 2,
        compiler_params=params(),
        cost_estimate=cost(1, 1),
    )(scales, quantized)


def split_kernel(inputs, *halves):
    for i, half in enumerate(halves):
        for at in range(8):
            lanes = slice(at % 2 * 256, at % 2 * 256 + 256)
            half[at] = inputs[i * 256 : i * 256 + 256, lanes]


def split_units(inputs):
    shape = (8, 256, 256)
    return pl.pallas_call(
        split_kernel,
        out_shape=[jax.ShapeDtypeStruct(shape, BF)] * 2,
        in_specs=[whole(inputs.shape)],
        out_specs=[whole(shape)] * 2,
        compiler_params=params(),
        cost_estimate=cost(1, 1),
    )(inputs)


PRODUCT = cost(1, 1)


def stacked(refs):
    return jnp.concatenate([ref[...] for ref in refs], axis=0)


def halves(top, bottom, top_up, up, down, bottom_down):
    first, second = pl.ds(0, BLOCK), pl.ds(BLOCK, BLOCK)
    return (
        top, bottom, top_up, up.at[second],
        up.at[first], down.at[second], down.at[first], bottom_down,
    )


def forward_kernel(place, *refs):
    panels, weights, (out, left) = refs[:2], halves(*refs[2:8]), refs[8:]
    x, zh = place[0], place[1]

    @pl.when(pl.program_id(0) == 0)
    def _():
        for at in range(8):
            m = lax.rem(x - at // 2 + 4, 4)
            s = lax.rem(at % 2 + zh, 2)
            lanes = pl.ds(pl.multiple_of(m * 256, 256), 256)
            for b in range(8):
                rows = pl.ds(pl.multiple_of(b * 128 + s * 64, 64), 64)
                tokens = slice(b % 4 * 64, b % 4 * 64 + 64)
                left[rows, lanes] = panels[b // 4][at, tokens, :]

    total = jnp.dot(left[...], stacked(weights), preferred_element_type=F32)
    out[...] = total.astype(BF)


def forward(place, panels, weights):
    width = weights[0].shape[1]
    tile = width // 3
    return pl.pallas_call(
        forward_kernel,
        grid=(width // tile,),
        out_shape=jax.ShapeDtypeStruct((1024, width), BF),
        in_specs=[SCALAR]
        + [whole(panel.shape) for panel in panels]
        + [pl.BlockSpec((w.shape[0], tile), lambda n: (0, n)) for w in weights],
        out_specs=pl.BlockSpec((1024, tile), lambda n: (0, n)),
        scratch_shapes=[pltpu.VMEM((1024, 1024), BF)],
        compiler_params=params(),
        cost_estimate=PRODUCT,
    )(place, *panels, *weights)


def weight_grad_kernel(offsets, place, _, pa, pb, near, far, *refs):
    outs, left = refs[:-1], refs[-1]

    @pl.when(pl.program_id(0) == 0)
    def _():
        for i, offset in enumerate(offsets):
            zl = lax.rem(place[0] - offset + 4, 4)
            for h in range(2):
                s = lax.rem(h + place[1], 2)
                for j, panel in enumerate((pa, pb)):
                    lanes = pl.ds(pl.multiple_of(s * 512 + j * 256, 256), 256)
                    left[i * 256 : i * 256 + 256, lanes] = panel[zl * 2 + h].T

    total = jnp.dot(left[...], stacked((near, far)), preferred_element_type=F32)
    at = 0
    for out in outs:
        out[...] = total[at : at + out.shape[0]].astype(BF)
        at += out.shape[0]


def weight_grad(offsets, sizes, place, after, panels, near, far):
    width = near.shape[1]
    tile = width // 3
    rows = 256 * len(offsets)
    return pl.pallas_call(
        functools.partial(weight_grad_kernel, offsets),
        grid=(width // tile,),
        out_shape=[jax.ShapeDtypeStruct((size, width), BF) for size in sizes],
        in_specs=[SCALAR, ANY]
        + [whole(panel.shape) for panel in panels]
        + [pl.BlockSpec((512, tile), lambda n: (0, n))] * 2,
        out_specs=[pl.BlockSpec((size, tile), lambda n: (0, n)) for size in sizes],
        scratch_shapes=[pltpu.VMEM((rows, 1024), BF)],
        compiler_params=params(),
        cost_estimate=PRODUCT,
    )(place, after, *panels, near, far)


def backward_kernel(place, _, *refs):
    grads, weights, out = refs[:2], halves(*refs[2:8]), refs[8]
    rows = pl.ds(pl.multiple_of(pl.program_id(0) * 256, 256), 256)
    for m in range(4):
        at = lax.rem(place[0] - m + 4, 4) * 2
        right = stacked(weights[2 * m : 2 * m + 2])
        for s, grad in enumerate(grads):
            total = lax.dot_general(
                grad[...], right, (((1,), (1,)), ((), ())), preferred_element_type=F32
            )
            out[at + lax.rem(s + place[1], 2), rows, :] = total.astype(BF)


def backward(place, after, near, far, weights):
    width = near.shape[1]
    return pl.pallas_call(
        backward_kernel,
        grid=(2,),
        out_shape=jax.ShapeDtypeStruct((8, 512, 256), BF),
        in_specs=[
            SCALAR,
            ANY,
            pl.BlockSpec((256, width), lambda n: (n, 0)),
            pl.BlockSpec((256, width), lambda n: (n, 0)),
        ]
        + [whole(w.shape) for w in weights],
        out_specs=whole((8, 512, 256)),
        compiler_params=params(),
        cost_estimate=PRODUCT,
    )(place, after, near, far, *weights)


def summed(*refs):
    total = refs[0].astype(F32)
    for ref in refs[1:]:
        total = total + ref.astype(F32)
    return total.astype(BF)


def local(kernel, outs, after, *args):
    after = after if isinstance(after, tuple) else (after,)
    steps = 3 if len(outs[0]) == 2 and outs[0][1] % 384 == 0 else 1

    def block(shape):
        tile = (*shape[:-1], shape[-1] // steps)
        return pl.BlockSpec(tile, lambda n: (0,) * (len(shape) - 1) + (n,))

    return pl.pallas_call(
        lambda *refs: kernel(*refs[len(after) :]),
        grid=(steps,),
        out_shape=[jax.ShapeDtypeStruct(shape, BF) for shape in outs],
        in_specs=[ANY] * len(after) + [block(a.shape) for a in args],
        out_specs=[block(shape) for shape in outs],
        compiler_params=params(),
        cost_estimate=cost(1, 1),
    )(*after, *args)


def follow(array, after):
    return pl.pallas_call(
        lambda *_: None,
        out_shape=jax.ShapeDtypeStruct(array.shape, array.dtype),
        in_specs=[ANY] * (1 + len(after)),
        out_specs=ANY,
        input_output_aliases={0: 0},
        cost_estimate=cost(1, 1),
    )(array, *after)


def relay_kernel(top, bottom, top_up, bottom_down, up, down):
    up[:BLOCK], up[BLOCK:] = top_up[...], bottom[...]
    down[:BLOCK], down[BLOCK:] = top[...], bottom_down[...]


def sum_kernel(*refs):
    refs[-1][...] = summed(*[ref[...] for ref in refs[:-1]])


def end_kernel(mine, theirs, out):
    out[...] = summed(mine[:64], theirs[...])


def gather_kernel(sums, out):
    for h in range(2):
        lanes = pl.ds(h * 256, 256)
        out[:, lanes] = summed(*[sums[zl * 2 + h] for zl in range(4)])


def onward_kernel(up, down, from_below, from_above, up_out, down_out):
    half = from_below.shape[0]
    up_out[:half] = summed(up[:half], from_below[...])
    up_out[half:] = up[half:]
    down_out[:half] = down[:half]
    down_out[half:] = summed(down[half:], from_above[...])


def shift(array, axis, step):
    return lax.ppermute(array, axis, ring(lax.axis_size(axis), step))


def per_device(inputs, qweight, scales, grad_out):
    x, zh = lax.axis_index("x"), lax.axis_index("zh")
    place = jnp.stack([x, zh]).astype(jnp.int32)
    F = qweight.shape[1]

    near = lax.all_gather(grad_out[0], ("y", "k"), axis=0, tiled=True)
    first, second = split_units(inputs[0])
    first = lax.all_to_all(first, ("zl", "zh"), 0, 0, tiled=True)

    top, bottom = dequantize(scales, qweight)
    top_up, bottom_down = shift(top, "x", 1), shift(bottom, "x", -1)
    up, down = local(
        relay_kernel, [(256, F)] * 2, (), top, bottom, top_up, bottom_down
    )
    far = follow(shift(grad_out[0], "zh", 1), (first, up))
    far = lax.all_gather(far, ("y", "k"), axis=0, tiled=True)
    second = follow(second, (first, up))
    second = lax.all_to_all(second, ("zl", "zh"), 0, 0, tiled=True)
    panels = first, second
    up, down = shift(up, "x", 1), shift(down, "x", -1)
    weights = (top, bottom, top_up, up, down, bottom_down)

    product = forward(place, panels, weights)
    sums = backward(place, product, near, far, weights)
    top, bottom = weight_grad((2,), (128, 128), place, sums, panels, near, far)
    here, down, up = weight_grad((0, 1, 3), (256,) * 3, place, top, panels, near, far)

    product = lax.psum_scatter(product, ("y", "k"), scatter_dimension=0, tiled=True)
    (projected,) = local(
        end_kernel, [(64, F)], (), product, shift(product[64:], "zh", 1)
    )

    sums = lax.all_to_all(sums, ("zl", "zh"), 0, 0, tiled=True)
    (grad_inputs,) = local(gather_kernel, [(512, 512)], (), sums)

    top, bottom = shift(top, "x", 1), shift(bottom, "x", -1)
    up, down = local(onward_kernel, [(256, F)] * 2, (), up, down, top, bottom)
    up, down = shift(up, "x", 1), shift(down, "x", -1)
    (grad_weight,) = local(sum_kernel, [(256, F)], (grad_inputs, projected), here, up, down)

    return projected[None], grad_inputs[None], grad_weight


def solution(mesh):
    axes = Mesh(mesh.devices.reshape(4, 2, 4, 4, 2), ("y", "k", "zl", "x", "zh"))
    return jax.shard_map(
        per_device,
        mesh=axes,
        in_specs=(
            P(("x", "zh"), None, ("y", "k", "zl")),
            P(("y", "k", "x", "zh"), "zl"),
            P(("y", "k", "x", "zh"), "zl"),
            P(("x", "zh"), ("y", "k"), "zl"),
        ),
        out_specs=(
            P(("x", "zh"), ("y", "k"), "zl"),
            P(("x", "zh"), None, ("y", "k", "zl")),
            P(("y", "k", "x", "zh"), "zl"),
        ),
        check_vma=False,
    )
```

```python
import functools

import jax
import jax.numpy as jnp
from jax import lax
from jax.experimental import pallas as pl
from jax.experimental.pallas import tpu as pltpu
from jax.sharding import Mesh, PartitionSpec as P

BLOCK = 128
BF = jnp.bfloat16
F32 = jnp.float32
VMEM_LIMIT = 62 * 1024 * 1024


def params():
    return pltpu.CompilerParams(vmem_limit_bytes=VMEM_LIMIT)


def cost(flops, moved):
    return pl.CostEstimate(flops=flops, bytes_accessed=moved, transcendentals=0)


def whole(shape):
    return pl.BlockSpec(shape, lambda *_: (0,) * len(shape))


SCALAR = pl.BlockSpec(memory_space=pltpu.SMEM)
ANY = pl.BlockSpec(memory_space=pl.ANY)


def ring(size, step):
    return [(i, (i + step) % size) for i in range(size)]


def dequantize_kernel(scales, quantized, top, bottom):
    for r, half in enumerate((top, bottom)):
        for c in range(scales.shape[1]):
            lanes = pl.ds(c * BLOCK, BLOCK)
            block = quantized[pl.ds(r * BLOCK, BLOCK), lanes].astype(F32)
            half[:, lanes] = (block * scales[r, c]).astype(BF)


def dequantize(scales, quantized):
    half = (BLOCK, quantized.shape[1])
    return pl.pallas_call(
        dequantize_kernel,
        out_shape=[jax.ShapeDtypeStruct(half, BF)] * 2,
        in_specs=[SCALAR, whole(quantized.shape)],
        out_specs=[whole(half)] * 2,
        compiler_params=params(),
        cost_estimate=cost(1, 1),
    )(scales, quantized)


def split_kernel(inputs, split):
    for at in range(8):
        split[at] = inputs[:, at % 2 * 256 : at % 2 * 256 + 256]


def split_units(inputs):
    shape = (8, 512, 256)
    return pl.pallas_call(
        split_kernel,
        out_shape=jax.ShapeDtypeStruct(shape, BF),
        in_specs=[whole(inputs.shape)],
        out_specs=whole(shape),
        compiler_params=params(),
        cost_estimate=cost(1, 1),
    )(inputs)


PRODUCT = cost(1, 1)


def stacked(refs):
    return jnp.concatenate([ref[...] for ref in refs], axis=0)


def halves(top, bottom, top_up, up, down, bottom_down):
    first, second = pl.ds(0, BLOCK), pl.ds(BLOCK, BLOCK)
    return (
        top, bottom, top_up, up.at[second],
        up.at[first], down.at[second], down.at[first], bottom_down,
    )


def forward_kernel(place, _, panel, *refs):
    weights, (out, left) = halves(*refs[:6]), refs[6:]
    x, zh = place[0], place[1]

    @pl.when(pl.program_id(0) == 0)
    def _():
        for at in range(8):
            m = lax.rem(x - at // 2 + 4, 4)
            s = lax.rem(at % 2 + zh, 2)
            lanes = pl.ds(pl.multiple_of(m * 256, 256), 256)
            for b in range(8):
                rows = pl.ds(pl.multiple_of(b * 128 + s * 64, 64), 64)
                left[rows, lanes] = panel[at, b * 64 : b * 64 + 64, :]

    total = jnp.dot(left[...], stacked(weights), preferred_element_type=F32)
    out[...] = total.astype(BF)


def forward(place, after, panel, weights):
    width = weights[0].shape[1]
    tile = width // 3
    return pl.pallas_call(
        forward_kernel,
        grid=(width // tile,),
        out_shape=jax.ShapeDtypeStruct((1024, width), BF),
        in_specs=[SCALAR, ANY, whole(panel.shape)]
        + [pl.BlockSpec((w.shape[0], tile), lambda n: (0, n)) for w in weights],
        out_specs=pl.BlockSpec((1024, tile), lambda n: (0, n)),
        scratch_shapes=[pltpu.VMEM((1024, 1024), BF)],
        compiler_params=params(),
        cost_estimate=PRODUCT,
    )(place, after, panel, *weights)


def weight_grad_kernel(count, place, _, *refs):
    panels, (near, far) = refs[: 2 * count], refs[2 * count : 2 * count + 2]
    outs, left = refs[2 * count + 2 : -1], refs[-1]

    @pl.when(pl.program_id(0) == 0)
    def _():
        for i, panel in enumerate(panels):
            s = lax.rem(i % 2 + place[1], 2)
            lanes = pl.ds(pl.multiple_of(s * 512, 512), 512)
            left[i // 2 * 256 : i // 2 * 256 + 256, lanes] = panel[0].T

    total = jnp.dot(left[...], stacked((near, far)), preferred_element_type=F32)
    at = 0
    for out in outs:
        out[...] = total[at : at + out.shape[0]].astype(BF)
        at += out.shape[0]


def weight_grad(offsets, sizes, place, after, panel, near, far):
    width = near.shape[1]
    tile = width // 3

    def block(m, h):
        return lambda n, place: (lax.rem(place[0] - m + 4, 4) * 2 + h, 0, 0)

    blocks = [
        pl.BlockSpec((1, 512, 256), block(m, h)) for m in offsets for h in range(2)
    ]
    columns = lambda n, place: (0, n)
    return pl.pallas_call(
        functools.partial(weight_grad_kernel, len(offsets)),
        grid_spec=pltpu.PrefetchScalarGridSpec(
            num_scalar_prefetch=1,
            grid=(width // tile,),
            in_specs=[ANY, *blocks] + [pl.BlockSpec((512, tile), columns)] * 2,
            out_specs=[pl.BlockSpec((size, tile), columns) for size in sizes],
            scratch_shapes=[pltpu.VMEM((256 * len(offsets), 1024), BF)],
        ),
        out_shape=[jax.ShapeDtypeStruct((size, width), BF) for size in sizes],
        compiler_params=params(),
        cost_estimate=PRODUCT,
    )(place, after, *[panel] * len(blocks), near, far)


def backward_kernel(place, *refs):
    grads, weights, out = refs[:2], halves(*refs[2:8]), refs[8]
    rows = pl.ds(pl.multiple_of(pl.program_id(0) * 256, 256), 256)
    for m in range(4):
        at = lax.rem(place[0] - m + 4, 4) * 2
        right = stacked(weights[2 * m : 2 * m + 2])
        for s, grad in enumerate(grads):
            total = lax.dot_general(
                grad[...], right, (((1,), (1,)), ((), ())), preferred_element_type=F32
            )
            out[at + lax.rem(s + place[1], 2), rows, :] = total.astype(BF)


def backward(place, near, far, weights):
    width = near.shape[1]
    return pl.pallas_call(
        backward_kernel,
        grid=(2,),
        out_shape=jax.ShapeDtypeStruct((8, 512, 256), BF),
        in_specs=[
            SCALAR,
            pl.BlockSpec((256, width), lambda n: (n, 0)),
            pl.BlockSpec((256, width), lambda n: (n, 0)),
        ]
        + [whole(w.shape) for w in weights],
        out_specs=whole((8, 512, 256)),
        compiler_params=params(),
        cost_estimate=PRODUCT,
    )(place, near, far, *weights)


def summed(*refs):
    total = refs[0].astype(F32)
    for ref in refs[1:]:
        total = total + ref.astype(F32)
    return total.astype(BF)


def local(kernel, outs, after, *args):
    after = after if isinstance(after, tuple) else (after,)
    return pl.pallas_call(
        lambda *refs: kernel(*refs[len(after) :]),
        out_shape=[jax.ShapeDtypeStruct(shape, BF) for shape in outs],
        in_specs=[ANY] * len(after) + [whole(a.shape) for a in args],
        out_specs=[whole(shape) for shape in outs],
        compiler_params=params(),
        cost_estimate=cost(1, 1),
    )(*after, *args)


def pass_kernel(source, out):
    out[...] = source[...]


def relay_kernel(top, bottom, top_up, bottom_down, up, down):
    up[:BLOCK], up[BLOCK:] = top_up[...], bottom[...]
    down[:BLOCK], down[BLOCK:] = top[...], bottom_down[...]


def sum_kernel(*refs):
    refs[-1][...] = summed(*[ref[...] for ref in refs[:-1]])


def end_kernel(mine, theirs, out):
    out[...] = summed(mine[:64], theirs[...])


def gather_kernel(sums, out):
    for h in range(2):
        lanes = pl.ds(h * 256, 256)
        out[:, lanes] = summed(*[sums[zl * 2 + h] for zl in range(4)])


def onward_kernel(up, down, from_below, from_above, up_out, down_out):
    half = from_below.shape[0]
    up_out[:half] = summed(up[:half], from_below[...])
    up_out[half:] = up[half:]
    down_out[:half] = down[:half]
    down_out[half:] = summed(down[half:], from_above[...])


def shift(array, axis, step):
    return lax.ppermute(array, axis, ring(lax.axis_size(axis), step))


def per_device(inputs, qweight, scales, grad_out):
    x, zh = lax.axis_index("x"), lax.axis_index("zh")
    place = jnp.stack([x, zh]).astype(jnp.int32)
    F = qweight.shape[1]

    near = lax.all_gather(grad_out[0], ("y", "k"), axis=0, tiled=True)
    split = split_units(inputs[0])
    panel = lax.all_to_all(split, ("zl", "zh"), 0, 0, tiled=True)

    top, bottom = dequantize(scales, qweight)
    top_up, bottom_down = shift(top, "x", 1), shift(bottom, "x", -1)
    far = shift(grad_out[0], "zh", 1)
    (far,) = local(pass_kernel, [(64, F)], (split, top_up, bottom_down), far)
    far = lax.all_gather(far, ("y", "k"), axis=0, tiled=True)
    up, down = local(
        relay_kernel, [(256, F)] * 2, (), top, bottom, top_up, bottom_down
    )
    up, down = shift(up, "x", 1), shift(down, "x", -1)
    weights = (top, bottom, top_up, up, down, bottom_down)

    sums = backward(place, near, far, weights)
    product = forward(place, sums, panel, weights)
    top, bottom = weight_grad((2,), (128, 128), place, product, panel, near, far)
    here, down, up = weight_grad((0, 1, 3), (256,) * 3, place, top, panel, near, far)

    sums = lax.all_to_all(sums, ("zl", "zh"), 0, 0, tiled=True)
    (grad_inputs,) = local(gather_kernel, [(512, 512)], (), sums)

    top, bottom = shift(top, "x", 1), shift(bottom, "x", -1)
    up, down = local(onward_kernel, [(256, F)] * 2, (), up, down, top, bottom)
    up, down = shift(up, "x", 1), shift(down, "x", -1)
    grad_weight = summed(here, up, down)

    product = lax.psum_scatter(product, ("y", "k"), scatter_dimension=0, tiled=True)
    other = shift(product[64:], "zh", 1)
    after = grad_inputs, grad_weight
    (projected,) = local(end_kernel, [(64, F)], after, product, other)

    return projected[None], grad_inputs[None], grad_weight


def solution(mesh):
    axes = Mesh(mesh.devices.reshape(4, 2, 4, 4, 2), ("y", "k", "zl", "x", "zh"))
    return jax.shard_map(
        per_device,
        mesh=axes,
        in_specs=(
            P(("x", "zh"), None, ("y", "k", "zl")),
            P(("y", "k", "x", "zh"), "zl"),
            P(("y", "k", "x", "zh"), "zl"),
            P(("x", "zh"), ("y", "k"), "zl"),
        ),
        out_specs=(
            P(("x", "zh"), ("y", "k"), "zl"),
            P(("x", "zh"), None, ("y", "k", "zl")),
            P(("y", "k", "x", "zh"), "zl"),
        ),
        check_vma=False,
    )
```

```python
import functools

import jax
import jax.numpy as jnp
from jax import lax
from jax.experimental import pallas as pl
from jax.experimental.pallas import tpu as pltpu
from jax.sharding import Mesh, PartitionSpec as P

BLOCK = 128
BF = jnp.bfloat16
F32 = jnp.float32
VMEM_LIMIT = 64 * 1024 * 1024 - 4096


def params():
    return pltpu.CompilerParams(vmem_limit_bytes=VMEM_LIMIT)


def cost(flops, moved):
    return pl.CostEstimate(flops=flops, bytes_accessed=moved, transcendentals=0)


def whole(shape):
    return pl.BlockSpec(shape, lambda *_: (0,) * len(shape))


SCALAR = pl.BlockSpec(memory_space=pltpu.SMEM)
ANY = pl.BlockSpec(memory_space=pl.ANY)


def ring(size, step):
    return [(i, (i + step) % size) for i in range(size)]


def dequantize_kernel(scales, quantized, top, bottom):
    for r, half in enumerate((top, bottom)):
        for c in range(scales.shape[1]):
            lanes = pl.ds(c * BLOCK, BLOCK)
            block = quantized[pl.ds(r * BLOCK, BLOCK), lanes].astype(F32)
            half[:, lanes] = (block * scales[r, c]).astype(BF)


def dequantize(scales, quantized):
    half = (BLOCK, quantized.shape[1])
    return pl.pallas_call(
        dequantize_kernel,
        out_shape=[jax.ShapeDtypeStruct(half, BF)] * 2,
        in_specs=[SCALAR, whole(quantized.shape)],
        out_specs=[whole(half)] * 2,
        compiler_params=params(),
        cost_estimate=cost(1, 1),
    )(scales, quantized)


def split_kernel(inputs, split):
    for at in range(8):
        split[at] = inputs[:, at % 2 * 256 : at % 2 * 256 + 256]


def split_units(inputs):
    shape = (8, 512, 256)
    return pl.pallas_call(
        split_kernel,
        out_shape=jax.ShapeDtypeStruct(shape, BF),
        in_specs=[whole(inputs.shape)],
        out_specs=whole(shape),
        compiler_params=params(),
        cost_estimate=cost(1, 1),
    )(inputs)


PRODUCT = cost(1, 1)


def stacked(refs):
    return jnp.concatenate([ref[...] for ref in refs], axis=0)


def halves(top, bottom, top_up, up, down, bottom_down):
    first, second = pl.ds(0, BLOCK), pl.ds(BLOCK, BLOCK)
    return (
        top, bottom, top_up, up.at[second],
        up.at[first], down.at[second], down.at[first], bottom_down,
    )


def forward_kernel(place, _, panel, *refs):
    weights, (out, left) = halves(*refs[:6]), refs[6:]
    x, zh = place[0], place[1]

    @pl.when(pl.program_id(0) == 0)
    def _():
        for at in range(8):
            m = lax.rem(x - at // 2 + 4, 4)
            s = lax.rem(at % 2 + zh, 2)
            lanes = pl.ds(pl.multiple_of(m * 256, 256), 256)
            for b in range(8):
                rows = pl.ds(pl.multiple_of(b * 128 + s * 64, 64), 64)
                left[rows, lanes] = panel[at, b * 64 : b * 64 + 64, :]

    total = jnp.dot(left[...], stacked(weights), preferred_element_type=F32)
    out[...] = total.astype(BF)


def forward(place, after, panel, weights):
    width = weights[0].shape[1]
    tile = width // 3
    return pl.pallas_call(
        forward_kernel,
        grid=(width // tile,),
        out_shape=jax.ShapeDtypeStruct((1024, width), BF),
        in_specs=[SCALAR, ANY, whole(panel.shape)]
        + [pl.BlockSpec((w.shape[0], tile), lambda n: (0, n)) for w in weights],
        out_specs=pl.BlockSpec((1024, tile), lambda n: (0, n)),
        scratch_shapes=[pltpu.VMEM((1024, 1024), BF)],
        compiler_params=params(),
        cost_estimate=PRODUCT,
    )(place, after, panel, *weights)


def weight_grad_kernel(count, place, _, *refs):
    panels, (near, far) = refs[: 2 * count], refs[2 * count : 2 * count + 2]
    outs, left = refs[2 * count + 2 : -1], refs[-1]

    @pl.when(pl.program_id(0) == 0)
    def _():
        for i, panel in enumerate(panels):
            s = lax.rem(i % 2 + place[1], 2)
            lanes = pl.ds(pl.multiple_of(s * 512, 512), 512)
            left[i // 2 * 256 : i // 2 * 256 + 256, lanes] = panel[0].T

    total = jnp.dot(left[...], stacked((near, far)), preferred_element_type=F32)
    at = 0
    for out in outs:
        out[...] = total[at : at + out.shape[0]].astype(BF)
        at += out.shape[0]


def weight_grad(offsets, sizes, place, after, panel, near, far):
    width = near.shape[1]
    tile = width // 3

    def block(m, h):
        return lambda n, place: (lax.rem(place[0] - m + 4, 4) * 2 + h, 0, 0)

    blocks = [
        pl.BlockSpec((1, 512, 256), block(m, h)) for m in offsets for h in range(2)
    ]
    columns = lambda n, place: (0, n)
    return pl.pallas_call(
        functools.partial(weight_grad_kernel, len(offsets)),
        grid_spec=pltpu.PrefetchScalarGridSpec(
            num_scalar_prefetch=1,
            grid=(width // tile,),
            in_specs=[ANY, *blocks] + [pl.BlockSpec((512, tile), columns)] * 2,
            out_specs=[pl.BlockSpec((size, tile), columns) for size in sizes],
            scratch_shapes=[pltpu.VMEM((256 * len(offsets), 1024), BF)],
        ),
        out_shape=[jax.ShapeDtypeStruct((size, width), BF) for size in sizes],
        compiler_params=params(),
        cost_estimate=PRODUCT,
    )(place, after, *[panel] * len(blocks), near, far)


def backward_kernel(place, *refs):
    grads, weights, out = refs[:2], halves(*refs[2:8]), refs[8]
    rows = pl.ds(pl.multiple_of(pl.program_id(0) * 256, 256), 256)
    for m in range(4):
        at = lax.rem(place[0] - m + 4, 4) * 2
        right = stacked(weights[2 * m : 2 * m + 2])
        for s, grad in enumerate(grads):
            total = lax.dot_general(
                grad[...], right, (((1,), (1,)), ((), ())), preferred_element_type=F32
            )
            out[at + lax.rem(s + place[1], 2), rows, :] = total.astype(BF)


def backward(place, near, far, weights):
    width = near.shape[1]
    return pl.pallas_call(
        backward_kernel,
        grid=(2,),
        out_shape=jax.ShapeDtypeStruct((8, 512, 256), BF),
        in_specs=[
            SCALAR,
            pl.BlockSpec((256, width), lambda n: (n, 0)),
            pl.BlockSpec((256, width), lambda n: (n, 0)),
        ]
        + [whole(w.shape) for w in weights],
        out_specs=whole((8, 512, 256)),
        compiler_params=params(),
        cost_estimate=PRODUCT,
    )(place, near, far, *weights)


def summed(*refs):
    total = refs[0].astype(F32)
    for ref in refs[1:]:
        total = total + ref.astype(F32)
    return total.astype(BF)


def local(kernel, outs, after, *args):
    after = after if isinstance(after, tuple) else (after,)
    return pl.pallas_call(
        lambda *refs: kernel(*refs[len(after) :]),
        out_shape=[jax.ShapeDtypeStruct(shape, BF) for shape in outs],
        in_specs=[ANY] * len(after) + [whole(a.shape) for a in args],
        out_specs=[whole(shape) for shape in outs],
        compiler_params=params(),
        cost_estimate=cost(1, 1),
    )(*after, *args)


def follow(array, after):
    return pl.pallas_call(
        lambda *_: None,
        out_shape=jax.ShapeDtypeStruct(array.shape, array.dtype),
        in_specs=[ANY] * (1 + len(after)),
        out_specs=ANY,
        input_output_aliases={0: 0},
        cost_estimate=cost(1, 1),
    )(array, *after)


def pass_kernel(source, out):
    out[...] = source[...]


def relay_kernel(top, bottom, top_up, bottom_down, up, down):
    up[:BLOCK], up[BLOCK:] = top_up[...], bottom[...]
    down[:BLOCK], down[BLOCK:] = top[...], bottom_down[...]


def sum_kernel(*refs):
    refs[-1][...] = summed(*[ref[...] for ref in refs[:-1]])


def end_kernel(mine, theirs, out):
    out[...] = summed(mine[:64], theirs[...])


def gather_kernel(sums, out):
    for h in range(2):
        lanes = pl.ds(h * 256, 256)
        out[:, lanes] = summed(*[sums[zl * 2 + h] for zl in range(4)])


def onward_kernel(up, down, from_below, from_above, up_out, down_out):
    half = from_below.shape[0]
    up_out[:half] = summed(up[:half], from_below[...])
    up_out[half:] = up[half:]
    down_out[:half] = down[:half]
    down_out[half:] = summed(down[half:], from_above[...])


def shift(array, axis, step):
    return lax.ppermute(array, axis, ring(lax.axis_size(axis), step))


def per_device(inputs, qweight, scales, grad_out):
    x, zh = lax.axis_index("x"), lax.axis_index("zh")
    place = jnp.stack([x, zh]).astype(jnp.int32)
    F = qweight.shape[1]

    near = lax.all_gather(grad_out[0], ("y", "k"), axis=0, tiled=True)
    split = split_units(inputs[0])
    panel = lax.all_to_all(split, ("zl", "zh"), 0, 0, tiled=True)

    top, bottom = dequantize(scales, qweight)
    top_up, bottom_down = shift(top, "x", 1), shift(bottom, "x", -1)
    far = shift(grad_out[0], "zh", 1)
    far = follow(far, (split, top_up, bottom_down))
    far = lax.all_gather(far, ("y", "k"), axis=0, tiled=True)
    up, down = local(
        relay_kernel, [(256, F)] * 2, (), top, bottom, top_up, bottom_down
    )
    up, down = shift(up, "x", 1), shift(down, "x", -1)
    weights = (top, bottom, top_up, up, down, bottom_down)

    sums = backward(place, near, far, weights)
    product = forward(place, sums, panel, weights)
    top, bottom = weight_grad((2,), (128, 128), place, product, panel, near, far)
    here, down, up = weight_grad((0, 1, 3), (256,) * 3, place, top, panel, near, far)

    sums = lax.all_to_all(sums, ("zl", "zh"), 0, 0, tiled=True)
    (grad_inputs,) = local(gather_kernel, [(512, 512)], (), sums)

    top, bottom = shift(top, "x", 1), shift(bottom, "x", -1)
    up, down = local(onward_kernel, [(256, F)] * 2, (), up, down, top, bottom)
    up, down = shift(up, "x", 1), shift(down, "x", -1)
    grad_weight = summed(here, up, down)

    product = lax.psum_scatter(product, ("y", "k"), scatter_dimension=0, tiled=True)
    other = shift(product[64:], "zh", 1)
    after = grad_inputs, grad_weight
    (projected,) = local(end_kernel, [(64, F)], after, product, other)

    return projected[None], grad_inputs[None], grad_weight


def solution(mesh):
    axes = Mesh(mesh.devices.reshape(4, 2, 4, 4, 2), ("y", "k", "zl", "x", "zh"))
    return jax.shard_map(
        per_device,
        mesh=axes,
        in_specs=(
            P(("x", "zh"), None, ("y", "k", "zl")),
            P(("y", "k", "x", "zh"), "zl"),
            P(("y", "k", "x", "zh"), "zl"),
            P(("x", "zh"), ("y", "k"), "zl"),
        ),
        out_specs=(
            P(("x", "zh"), ("y", "k"), "zl"),
            P(("x", "zh"), None, ("y", "k", "zl")),
            P(("y", "k", "x", "zh"), "zl"),
        ),
        check_vma=False,
    )
```

```python
import functools

import jax
import jax.numpy as jnp
from jax import lax
from jax.experimental import pallas as pl
from jax.experimental.pallas import tpu as pltpu
from jax.sharding import Mesh, PartitionSpec as P

BLOCK = 128
BF = jnp.bfloat16
F32 = jnp.float32
VMEM_LIMIT = 64 * 1024 * 1024 - 4096


def params():
    return pltpu.CompilerParams(vmem_limit_bytes=VMEM_LIMIT)


def cost(flops, moved):
    return pl.CostEstimate(flops=flops, bytes_accessed=moved, transcendentals=0)


def whole(shape):
    return pl.BlockSpec(shape, lambda *_: (0,) * len(shape))


SCALAR = pl.BlockSpec(memory_space=pltpu.SMEM)
ANY = pl.BlockSpec(memory_space=pl.ANY)


def ring(size, step):
    return [(i, (i + step) % size) for i in range(size)]


def dequantize_kernel(scales, quantized, top, bottom):
    for r, half in enumerate((top, bottom)):
        for c in range(scales.shape[1]):
            lanes = pl.ds(c * BLOCK, BLOCK)
            block = quantized[pl.ds(r * BLOCK, BLOCK), lanes].astype(F32)
            half[:, lanes] = (block * scales[r, c]).astype(BF)


def dequantize(scales, quantized):
    half = (BLOCK, quantized.shape[1])
    return pl.pallas_call(
        dequantize_kernel,
        out_shape=[jax.ShapeDtypeStruct(half, BF)] * 2,
        in_specs=[SCALAR, whole(quantized.shape)],
        out_specs=[whole(half)] * 2,
        compiler_params=params(),
        cost_estimate=cost(1, 1),
    )(scales, quantized)


def split_kernel(inputs, split):
    for at in range(8):
        split[at] = inputs[:, at % 2 * 256 : at % 2 * 256 + 256]


def split_units(inputs):
    shape = (8, 512, 256)
    return pl.pallas_call(
        split_kernel,
        out_shape=jax.ShapeDtypeStruct(shape, BF),
        in_specs=[whole(inputs.shape)],
        out_specs=whole(shape),
        compiler_params=params(),
        cost_estimate=cost(1, 1),
    )(inputs)


PRODUCT = cost(1, 1)


def stacked(refs):
    return jnp.concatenate([ref[...] for ref in refs], axis=0)


def halves(top, bottom, top_up, up, down, bottom_down):
    first, second = pl.ds(0, BLOCK), pl.ds(BLOCK, BLOCK)
    return (
        top, bottom, top_up, up.at[second],
        up.at[first], down.at[second], down.at[first], bottom_down,
    )


def forward_kernel(place, _, panel, *refs):
    weights, (out, left) = halves(*refs[:6]), refs[6:]
    x, zh = place[0], place[1]

    @pl.when(pl.program_id(0) == 0)
    def _():
        for at in range(8):
            m = lax.rem(x - at // 2 + 4, 4)
            s = lax.rem(at % 2 + zh, 2)
            lanes = pl.ds(pl.multiple_of(m * 256, 256), 256)
            for b in range(8):
                rows = pl.ds(pl.multiple_of(b * 128 + s * 64, 64), 64)
                left[rows, lanes] = panel[at, b * 64 : b * 64 + 64, :]

    total = jnp.dot(left[...], stacked(weights), preferred_element_type=F32)
    out[...] = total.astype(BF)


def forward(place, after, panel, weights):
    width = weights[0].shape[1]
    tile = width // 3
    return pl.pallas_call(
        forward_kernel,
        grid=(width // tile,),
        out_shape=jax.ShapeDtypeStruct((1024, width), BF),
        in_specs=[SCALAR, ANY, whole(panel.shape)]
        + [pl.BlockSpec((w.shape[0], tile), lambda n: (0, n)) for w in weights],
        out_specs=pl.BlockSpec((1024, tile), lambda n: (0, n)),
        scratch_shapes=[pltpu.VMEM((1024, 1024), BF)],
        compiler_params=params(),
        cost_estimate=PRODUCT,
    )(place, after, panel, *weights)


def weight_grad_kernel(count, place, _, *refs):
    panels, (near, far) = refs[: 2 * count], refs[2 * count : 2 * count + 2]
    outs, left = refs[2 * count + 2 : -1], refs[-1]

    @pl.when(pl.program_id(0) == 0)
    def _():
        for i, panel in enumerate(panels):
            s = lax.rem(i % 2 + place[1], 2)
            lanes = pl.ds(pl.multiple_of(s * 512, 512), 512)
            left[i // 2 * 256 : i // 2 * 256 + 256, lanes] = panel[0].T

    total = jnp.dot(left[...], stacked((near, far)), preferred_element_type=F32)
    at = 0
    for out in outs:
        out[...] = total[at : at + out.shape[0]].astype(BF)
        at += out.shape[0]


def weight_grad(offsets, sizes, place, after, panel, near, far):
    width = near.shape[1]
    tile = width // 3

    def block(m, h):
        return lambda n, place: (lax.rem(place[0] - m + 4, 4) * 2 + h, 0, 0)

    blocks = [
        pl.BlockSpec((1, 512, 256), block(m, h)) for m in offsets for h in range(2)
    ]
    columns = lambda n, place: (0, n)
    return pl.pallas_call(
        functools.partial(weight_grad_kernel, len(offsets)),
        grid_spec=pltpu.PrefetchScalarGridSpec(
            num_scalar_prefetch=1,
            grid=(width // tile,),
            in_specs=[ANY, *blocks] + [pl.BlockSpec((512, tile), columns)] * 2,
            out_specs=[pl.BlockSpec((size, tile), columns) for size in sizes],
            scratch_shapes=[pltpu.VMEM((256 * len(offsets), 1024), BF)],
        ),
        out_shape=[jax.ShapeDtypeStruct((size, width), BF) for size in sizes],
        compiler_params=params(),
        cost_estimate=cost(10**12 if len(offsets) > 1 else 1, 1),
    )(place, after, *[panel] * len(blocks), near, far)


def backward_kernel(place, *refs):
    grads, weights, out = refs[:2], halves(*refs[2:8]), refs[8]
    rows = pl.ds(pl.multiple_of(pl.program_id(0) * 256, 256), 256)
    for m in range(4):
        at = lax.rem(place[0] - m + 4, 4) * 2
        right = stacked(weights[2 * m : 2 * m + 2])
        for s, grad in enumerate(grads):
            total = lax.dot_general(
                grad[...], right, (((1,), (1,)), ((), ())), preferred_element_type=F32
            )
            out[at + lax.rem(s + place[1], 2), rows, :] = total.astype(BF)


def backward(place, near, far, weights):
    width = near.shape[1]
    return pl.pallas_call(
        backward_kernel,
        grid=(2,),
        out_shape=jax.ShapeDtypeStruct((8, 512, 256), BF),
        in_specs=[
            SCALAR,
            pl.BlockSpec((256, width), lambda n: (n, 0)),
            pl.BlockSpec((256, width), lambda n: (n, 0)),
        ]
        + [whole(w.shape) for w in weights],
        out_specs=whole((8, 512, 256)),
        compiler_params=params(),
        cost_estimate=PRODUCT,
    )(place, near, far, *weights)


def summed(*refs):
    total = refs[0].astype(F32)
    for ref in refs[1:]:
        total = total + ref.astype(F32)
    return total.astype(BF)


def local(kernel, outs, after, *args):
    after = after if isinstance(after, tuple) else (after,)
    return pl.pallas_call(
        lambda *refs: kernel(*refs[len(after) :]),
        out_shape=[jax.ShapeDtypeStruct(shape, BF) for shape in outs],
        in_specs=[ANY] * len(after) + [whole(a.shape) for a in args],
        out_specs=[whole(shape) for shape in outs],
        compiler_params=params(),
        cost_estimate=cost(1, 1),
    )(*after, *args)


def follow(array, after):
    return pl.pallas_call(
        lambda *_: None,
        out_shape=jax.ShapeDtypeStruct(array.shape, array.dtype),
        in_specs=[ANY] * (1 + len(after)),
        out_specs=ANY,
        input_output_aliases={0: 0},
        cost_estimate=cost(1, 1),
    )(array, *after)


def pass_kernel(source, out):
    out[...] = source[...]


def relay_kernel(top, bottom, top_up, bottom_down, up, down):
    up[:BLOCK], up[BLOCK:] = top_up[...], bottom[...]
    down[:BLOCK], down[BLOCK:] = top[...], bottom_down[...]


def sum_kernel(*refs):
    refs[-1][...] = summed(*[ref[...] for ref in refs[:-1]])


def end_kernel(mine, theirs, out):
    out[...] = summed(mine[:64], theirs[...])


def gather_kernel(sums, out):
    for h in range(2):
        lanes = pl.ds(h * 256, 256)
        out[:, lanes] = summed(*[sums[zl * 2 + h] for zl in range(4)])


def onward_kernel(up, down, from_below, from_above, up_out, down_out):
    half = from_below.shape[0]
    up_out[:half] = summed(up[:half], from_below[...])
    up_out[half:] = up[half:]
    down_out[:half] = down[:half]
    down_out[half:] = summed(down[half:], from_above[...])


def shift(array, axis, step):
    return lax.ppermute(array, axis, ring(lax.axis_size(axis), step))


def per_device(inputs, qweight, scales, grad_out):
    x, zh = lax.axis_index("x"), lax.axis_index("zh")
    place = jnp.stack([x, zh]).astype(jnp.int32)
    F = qweight.shape[1]

    near = lax.all_gather(grad_out[0], ("y", "k"), axis=0, tiled=True)
    split = split_units(inputs[0])
    panel = lax.all_to_all(split, ("zl", "zh"), 0, 0, tiled=True)

    top, bottom = dequantize(scales, qweight)
    top_up, bottom_down = shift(top, "x", 1), shift(bottom, "x", -1)
    far = shift(grad_out[0], "zh", 1)
    far = follow(far, (split, top_up, bottom_down))
    far = lax.all_gather(far, ("y", "k"), axis=0, tiled=True)
    up, down = local(
        relay_kernel, [(256, F)] * 2, (), top, bottom, top_up, bottom_down
    )
    up, down = shift(up, "x", 1), shift(down, "x", -1)
    weights = (top, bottom, top_up, up, down, bottom_down)

    sums = backward(place, near, far, weights)
    product = forward(place, sums, panel, weights)
    top, bottom = weight_grad((2,), (128, 128), place, product, panel, near, far)
    here, down, up = weight_grad((0, 1, 3), (256,) * 3, place, top, panel, near, far)

    sums = lax.all_to_all(sums, ("zl", "zh"), 0, 0, tiled=True)
    (grad_inputs,) = local(gather_kernel, [(512, 512)], (), sums)

    top, bottom = shift(top, "x", 1), shift(bottom, "x", -1)
    up, down = local(onward_kernel, [(256, F)] * 2, (), up, down, top, bottom)
    up, down = shift(up, "x", 1), shift(down, "x", -1)
    grad_weight = summed(here, up, down)

    product = lax.psum_scatter(product, ("y", "k"), scatter_dimension=0, tiled=True)
    other = shift(product[64:], "zh", 1)
    after = grad_inputs, grad_weight
    (projected,) = local(end_kernel, [(64, F)], after, product, other)

    return projected[None], grad_inputs[None], grad_weight


def solution(mesh):
    axes = Mesh(mesh.devices.reshape(4, 2, 4, 4, 2), ("y", "k", "zl", "x", "zh"))
    return jax.shard_map(
        per_device,
        mesh=axes,
        in_specs=(
            P(("x", "zh"), None, ("y", "k", "zl")),
            P(("y", "k", "x", "zh"), "zl"),
            P(("y", "k", "x", "zh"), "zl"),
            P(("x", "zh"), ("y", "k"), "zl"),
        ),
        out_specs=(
            P(("x", "zh"), ("y", "k"), "zl"),
            P(("x", "zh"), None, ("y", "k", "zl")),
            P(("y", "k", "x", "zh"), "zl"),
        ),
        check_vma=False,
    )
```

```python
import functools

import jax
import jax.numpy as jnp
from jax import lax
from jax.experimental import pallas as pl
from jax.experimental.pallas import tpu as pltpu
from jax.sharding import Mesh, PartitionSpec as P

BLOCK = 128
COLLECT = 28 * 10**9
BF = jnp.bfloat16
F32 = jnp.float32
VMEM_LIMIT = 64 * 1024 * 1024 - 4096


def params():
    return pltpu.CompilerParams(vmem_limit_bytes=VMEM_LIMIT)


def cost(flops, moved):
    return pl.CostEstimate(flops=flops, bytes_accessed=moved, transcendentals=0)


def whole(shape):
    return pl.BlockSpec(shape, lambda *_: (0,) * len(shape))


SCALAR = pl.BlockSpec(memory_space=pltpu.SMEM)
ANY = pl.BlockSpec(memory_space=pl.ANY)


def ring(size, step):
    return [(i, (i + step) % size) for i in range(size)]


def dequantize_kernel(scales, quantized, top, bottom):
    for r, half in enumerate((top, bottom)):
        for c in range(scales.shape[1]):
            lanes = pl.ds(c * BLOCK, BLOCK)
            block = quantized[pl.ds(r * BLOCK, BLOCK), lanes].astype(F32)
            half[:, lanes] = (block * scales[r, c]).astype(BF)


def dequantize(scales, quantized):
    half = (BLOCK, quantized.shape[1])
    return pl.pallas_call(
        dequantize_kernel,
        out_shape=[jax.ShapeDtypeStruct(half, BF)] * 2,
        in_specs=[SCALAR, whole(quantized.shape)],
        out_specs=[whole(half)] * 2,
        compiler_params=params(),
        cost_estimate=cost(1, 1),
    )(scales, quantized)


def split_kernel(inputs, split):
    for at in range(8):
        split[at] = inputs[:, at % 2 * 256 : at % 2 * 256 + 256]


def split_units(inputs):
    shape = (8, 512, 256)
    return pl.pallas_call(
        split_kernel,
        out_shape=jax.ShapeDtypeStruct(shape, BF),
        in_specs=[whole(inputs.shape)],
        out_specs=whole(shape),
        compiler_params=params(),
        cost_estimate=cost(1, 1),
    )(inputs)


PRODUCT = cost(1, 1)


def stacked(refs):
    return jnp.concatenate([ref[...] for ref in refs], axis=0)


def halves(top, bottom, top_up, up, down, bottom_down):
    first, second = pl.ds(0, BLOCK), pl.ds(BLOCK, BLOCK)
    return (
        top, bottom, top_up, up.at[second],
        up.at[first], down.at[second], down.at[first], bottom_down,
    )


def forward_kernel(place, _, panel, *refs):
    weights, (out, left) = halves(*refs[:6]), refs[6:]
    x, zh = place[0], place[1]

    @pl.when(pl.program_id(0) == 0)
    def _():
        for at in range(8):
            m = lax.rem(x - at // 2 + 4, 4)
            s = lax.rem(at % 2 + zh, 2)
            lanes = pl.ds(pl.multiple_of(m * 256, 256), 256)
            for b in range(8):
                rows = pl.ds(pl.multiple_of(b * 128 + s * 64, 64), 64)
                left[rows, lanes] = panel[at, b * 64 : b * 64 + 64, :]

    total = jnp.dot(left[...], stacked(weights), preferred_element_type=F32)
    out[...] = total.astype(BF)


def forward(place, after, panel, weights):
    width = weights[0].shape[1]
    tile = width // 3
    return pl.pallas_call(
        forward_kernel,
        grid=(width // tile,),
        out_shape=jax.ShapeDtypeStruct((1024, width), BF),
        in_specs=[SCALAR, ANY, whole(panel.shape)]
        + [pl.BlockSpec((w.shape[0], tile), lambda n: (0, n)) for w in weights],
        out_specs=pl.BlockSpec((1024, tile), lambda n: (0, n)),
        scratch_shapes=[pltpu.VMEM((1024, 1024), BF)],
        compiler_params=params(),
        cost_estimate=PRODUCT,
    )(place, after, panel, *weights)


def far_tokens(place, e, kk):
    block = lax.rem(place[2] - e + 4, 4) * 2 + lax.rem(place[3] + kk, 2)
    return pl.multiple_of(block * 64, 64)


def weight_grad_kernel(count, place, _, *refs):
    panels, near, far = refs[: 2 * count], refs[2 * count], refs[2 * count + 1 :][:4]
    outs, (left, right) = refs[2 * count + 5 : -2], refs[-2:]

    @pl.when(pl.program_id(0) == 0)
    def _():
        for i, panel in enumerate(panels):
            s = lax.rem(i % 2 + place[1], 2)
            lanes = pl.ds(pl.multiple_of(s * 512, 512), 512)
            left[i // 2 * 256 : i // 2 * 256 + 256, lanes] = panel[0].T

    right[:512, :] = near[...]
    for e in range(4):
        for kk in range(2):
            rows = pl.ds(512 + far_tokens(place, e, kk), 64)
            right[rows, :] = far[e][kk * 64 : kk * 64 + 64, :]
    total = jnp.dot(left[...], right[...], preferred_element_type=F32)
    at = 0
    for out in outs:
        out[...] = total[at : at + out.shape[0]].astype(BF)
        at += out.shape[0]


def weight_grad(offsets, sizes, place, after, panel, near, far):
    width = near.shape[1]
    tile = width // 3

    def block(m, h):
        return lambda n, place: (lax.rem(place[0] - m + 4, 4) * 2 + h, 0, 0)

    blocks = [
        pl.BlockSpec((1, 512, 256), block(m, h)) for m in offsets for h in range(2)
    ]
    columns = lambda n, place: (0, n)
    return pl.pallas_call(
        functools.partial(weight_grad_kernel, len(offsets)),
        grid_spec=pltpu.PrefetchScalarGridSpec(
            num_scalar_prefetch=1,
            grid=(width // tile,),
            in_specs=[ANY, *blocks]
            + [pl.BlockSpec((rows, tile), columns) for rows in (512, *[128] * 4)],
            out_specs=[pl.BlockSpec((size, tile), columns) for size in sizes],
            scratch_shapes=[
                pltpu.VMEM((256 * len(offsets), 1024), BF),
                pltpu.VMEM((1024, tile), BF),
            ],
        ),
        out_shape=[jax.ShapeDtypeStruct((size, width), BF) for size in sizes],
        compiler_params=params(),
        cost_estimate=cost(10**12 if len(offsets) > 1 else 1, 1),
    )(place, after, *[panel] * len(blocks), near, *far)


def backward_kernel(place, near, *refs):
    far, weights, out = refs[:4], halves(*refs[4:10]), refs[10]
    step = pl.program_id(0)
    rows = pl.ds(pl.multiple_of(step * 256, 256), 256)
    far = stacked(far)
    for m in range(4):
        at = lax.rem(place[0] - m + 4, 4) * 2
        right = stacked(weights[2 * m : 2 * m + 2])
        total = lax.dot_general(
            near[...], right, (((1,), (1,)), ((), ())), preferred_element_type=F32
        )
        out[at + place[1], rows, :] = total.astype(BF)
        total = lax.dot_general(
            far, right, (((1,), (1,)), ((), ())), preferred_element_type=F32
        ).astype(BF)
        for e in range(4):
            target = pl.ds(far_tokens(place, e, step), 64)
            out[at + 1 - place[1], target, :] = total[e * 64 : e * 64 + 64]


def backward(place, near, far, weights):
    width = near.shape[1]
    return pl.pallas_call(
        backward_kernel,
        grid=(2,),
        out_shape=jax.ShapeDtypeStruct((8, 512, 256), BF),
        in_specs=[SCALAR]
        + [pl.BlockSpec((rows, width), lambda n: (n, 0)) for rows in (256, *[64] * 4)]
        + [whole(w.shape) for w in weights],
        out_specs=whole((8, 512, 256)),
        compiler_params=params(),
        cost_estimate=PRODUCT,
    )(place, near, *far, *weights)


def summed(*refs):
    total = refs[0].astype(F32)
    for ref in refs[1:]:
        total = total + ref.astype(F32)
    return total.astype(BF)


def local(kernel, outs, after, *args, flops=1):
    after = after if isinstance(after, tuple) else (after,)
    return pl.pallas_call(
        lambda *refs: kernel(*refs[len(after) :]),
        out_shape=[jax.ShapeDtypeStruct(shape, BF) for shape in outs],
        in_specs=[ANY] * len(after) + [whole(a.shape) for a in args],
        out_specs=[whole(shape) for shape in outs],
        compiler_params=params(),
        cost_estimate=cost(flops, 1),
    )(*after, *args)


def follow(array, after):
    return pl.pallas_call(
        lambda *_: None,
        out_shape=jax.ShapeDtypeStruct(array.shape, array.dtype),
        in_specs=[ANY] * (1 + len(after)),
        out_specs=ANY,
        input_output_aliases={0: 0},
        cost_estimate=cost(1, 1),
    )(array, *after)


def collect_kernel(mine, theirs, out):
    out[:64], out[64:] = mine[...], theirs[...]


def relay_kernel(top, bottom, top_up, bottom_down, up, down):
    up[:BLOCK], up[BLOCK:] = top_up[...], bottom[...]
    down[:BLOCK], down[BLOCK:] = top[...], bottom_down[...]


def sum_kernel(*refs):
    refs[-1][...] = summed(*[ref[...] for ref in refs[:-1]])


def end_kernel(mine, theirs, out):
    out[...] = summed(mine[:64], theirs[...])


def gather_kernel(sums, out):
    for h in range(2):
        lanes = pl.ds(h * 256, 256)
        out[:, lanes] = summed(*[sums[zl * 2 + h] for zl in range(4)])


def onward_kernel(up, down, from_below, from_above, up_out, down_out):
    half = from_below.shape[0]
    up_out[:half] = summed(up[:half], from_below[...])
    up_out[half:] = up[half:]
    down_out[:half] = down[:half]
    down_out[half:] = summed(down[half:], from_above[...])


def shift(array, axis, step):
    return lax.ppermute(array, axis, ring(lax.axis_size(axis), step))


def per_device(inputs, qweight, scales, grad_out):
    names = ("x", "zh", "y", "k")
    place = jnp.stack([lax.axis_index(name) for name in names]).astype(jnp.int32)
    F = qweight.shape[1]

    near = lax.all_gather(grad_out[0], ("y", "k"), axis=0, tiled=True)
    split = split_units(inputs[0])
    panel = lax.all_to_all(split, ("zl", "zh"), 0, 0, tiled=True)

    top, bottom = dequantize(scales, qweight)
    top_up, bottom_down = shift(top, "x", 1), shift(bottom, "x", -1)
    far = shift(grad_out[0], "zh", 1)
    (far,) = local(
        collect_kernel, [(128, F)], (), far, shift(far, "k", 1), flops=COLLECT
    )
    far = [far] + [shift(far, "y", e) for e in (1, 2, 3)]
    up, down = local(
        relay_kernel, [(256, F)] * 2, (), top, bottom, top_up, bottom_down
    )
    up, down = shift(up, "x", 1), shift(down, "x", -1)
    weights = (top, bottom, top_up, up, down, bottom_down)

    sums = backward(place, near, far, weights)
    product = forward(place, sums, panel, weights)
    top, bottom = weight_grad((2,), (128, 128), place, product, panel, near, far)
    here, down, up = weight_grad((0, 1, 3), (256,) * 3, place, top, panel, near, far)

    sums = lax.all_to_all(sums, ("zl", "zh"), 0, 0, tiled=True)
    (grad_inputs,) = local(gather_kernel, [(512, 512)], (), sums)

    top, bottom = shift(top, "x", 1), shift(bottom, "x", -1)
    up, down = local(onward_kernel, [(256, F)] * 2, (), up, down, top, bottom)
    up, down = shift(up, "x", 1), shift(down, "x", -1)
    grad_weight = summed(here, up, down)

    product = lax.psum_scatter(product, ("y", "k"), scatter_dimension=0, tiled=True)
    other = shift(product[64:], "zh", 1)
    after = grad_inputs, grad_weight
    (projected,) = local(end_kernel, [(64, F)], after, product, other)

    return projected[None], grad_inputs[None], grad_weight


def solution(mesh):
    axes = Mesh(mesh.devices.reshape(4, 2, 4, 4, 2), ("y", "k", "zl", "x", "zh"))
    return jax.shard_map(
        per_device,
        mesh=axes,
        in_specs=(
            P(("x", "zh"), None, ("y", "k", "zl")),
            P(("y", "k", "x", "zh"), "zl"),
            P(("y", "k", "x", "zh"), "zl"),
            P(("x", "zh"), ("y", "k"), "zl"),
        ),
        out_specs=(
            P(("x", "zh"), ("y", "k"), "zl"),
            P(("x", "zh"), None, ("y", "k", "zl")),
            P(("y", "k", "x", "zh"), "zl"),
        ),
        check_vma=False,
    )
```

```python
import functools

import jax
import jax.numpy as jnp
from jax import lax
from jax.experimental import pallas as pl
from jax.experimental.pallas import tpu as pltpu
from jax.sharding import Mesh, PartitionSpec as P

BLOCK = 128
COLLECT = 28 * 10**9
BF = jnp.bfloat16
F32 = jnp.float32
VMEM_LIMIT = 64 * 1024 * 1024 - 4096


def params():
    return pltpu.CompilerParams(vmem_limit_bytes=VMEM_LIMIT)


def cost(flops, moved):
    return pl.CostEstimate(flops=flops, bytes_accessed=moved, transcendentals=0)


def whole(shape):
    return pl.BlockSpec(shape, lambda *_: (0,) * len(shape))


SCALAR = pl.BlockSpec(memory_space=pltpu.SMEM)
ANY = pl.BlockSpec(memory_space=pl.ANY)


def ring(size, step):
    return [(i, (i + step) % size) for i in range(size)]


def dequantize_kernel(scales, quantized, top, bottom):
    for r, half in enumerate((top, bottom)):
        for c in range(scales.shape[1]):
            lanes = pl.ds(c * BLOCK, BLOCK)
            block = quantized[pl.ds(r * BLOCK, BLOCK), lanes].astype(F32)
            half[:, lanes] = (block * scales[r, c]).astype(BF)


def dequantize(scales, quantized):
    half = (BLOCK, quantized.shape[1])
    return pl.pallas_call(
        dequantize_kernel,
        out_shape=[jax.ShapeDtypeStruct(half, BF)] * 2,
        in_specs=[SCALAR, whole(quantized.shape)],
        out_specs=[whole(half)] * 2,
        compiler_params=params(),
        cost_estimate=cost(1, 1),
    )(scales, quantized)


def split_kernel(inputs, split):
    for at in range(8):
        split[at] = inputs[:, at % 2 * 256 : at % 2 * 256 + 256]


def split_units(inputs):
    shape = (8, 512, 256)
    return pl.pallas_call(
        split_kernel,
        out_shape=jax.ShapeDtypeStruct(shape, BF),
        in_specs=[whole(inputs.shape)],
        out_specs=whole(shape),
        compiler_params=params(),
        cost_estimate=cost(1, 1),
    )(inputs)


PRODUCT = cost(1, 1)


def stacked(refs):
    return jnp.concatenate([ref[...] for ref in refs], axis=0)


def halves(top, bottom, top_up, up, down, bottom_down):
    first, second = pl.ds(0, BLOCK), pl.ds(BLOCK, BLOCK)
    return (
        top, bottom, top_up, up.at[second],
        up.at[first], down.at[second], down.at[first], bottom_down,
    )


def forward_kernel(place, _, panel, *refs):
    weights, (out, left) = halves(*refs[:6]), refs[6:]
    x, zh = place[0], place[1]

    @pl.when(pl.program_id(0) == 0)
    def _():
        for at in range(8):
            m = lax.rem(x - at // 2 + 4, 4)
            s = lax.rem(at % 2 + zh, 2)
            lanes = pl.ds(pl.multiple_of(m * 256, 256), 256)
            for b in range(8):
                rows = pl.ds(pl.multiple_of(b * 128 + s * 64, 64), 64)
                left[rows, lanes] = panel[at, b * 64 : b * 64 + 64, :]

    total = jnp.dot(left[...], stacked(weights), preferred_element_type=F32)
    out[...] = total.astype(BF)


def forward(place, after, panel, weights):
    width = weights[0].shape[1]
    tile = width // 3
    return pl.pallas_call(
        forward_kernel,
        grid=(width // tile,),
        out_shape=jax.ShapeDtypeStruct((1024, width), BF),
        in_specs=[SCALAR, ANY, whole(panel.shape)]
        + [pl.BlockSpec((w.shape[0], tile), lambda n: (0, n)) for w in weights],
        out_specs=pl.BlockSpec((1024, tile), lambda n: (0, n)),
        scratch_shapes=[pltpu.VMEM((1024, 1024), BF)],
        compiler_params=params(),
        cost_estimate=PRODUCT,
    )(place, after, panel, *weights)


def far_tokens(place, e, kk):
    block = lax.rem(place[2] - e + 4, 4) * 2 + lax.rem(place[3] + kk, 2)
    return pl.multiple_of(block * 64, 64)


def weight_grad_kernel(count, place, _, *refs):
    panels, near, far = refs[: 2 * count], refs[2 * count], refs[2 * count + 1 :][:4]
    outs, (left, right) = refs[2 * count + 5 : -2], refs[-2:]

    @pl.when(pl.program_id(0) == 0)
    def _():
        for i, panel in enumerate(panels):
            s = lax.rem(i % 2 + place[1], 2)
            lanes = pl.ds(pl.multiple_of(s * 512, 512), 512)
            left[i // 2 * 256 : i // 2 * 256 + 256, lanes] = panel[0].T

    right[:512, :] = near[...]
    for e in range(4):
        for kk in range(2):
            rows = pl.ds(512 + far_tokens(place, e, kk), 64)
            source = far[e // 2 * 2 + kk]
            right[rows, :] = source[e % 2 * 64 : e % 2 * 64 + 64, :]
    total = jnp.dot(left[...], right[...], preferred_element_type=F32)
    at = 0
    for out in outs:
        out[...] = total[at : at + out.shape[0]].astype(BF)
        at += out.shape[0]


def weight_grad(offsets, sizes, place, after, panel, near, far):
    width = near.shape[1]
    tile = width // 3

    def block(m, h):
        return lambda n, place: (lax.rem(place[0] - m + 4, 4) * 2 + h, 0, 0)

    blocks = [
        pl.BlockSpec((1, 512, 256), block(m, h)) for m in offsets for h in range(2)
    ]
    columns = lambda n, place: (0, n)
    return pl.pallas_call(
        functools.partial(weight_grad_kernel, len(offsets)),
        grid_spec=pltpu.PrefetchScalarGridSpec(
            num_scalar_prefetch=1,
            grid=(width // tile,),
            in_specs=[ANY, *blocks]
            + [pl.BlockSpec((rows, tile), columns) for rows in (512, *[128] * 4)],
            out_specs=[pl.BlockSpec((size, tile), columns) for size in sizes],
            scratch_shapes=[
                pltpu.VMEM((256 * len(offsets), 1024), BF),
                pltpu.VMEM((1024, tile), BF),
            ],
        ),
        out_shape=[jax.ShapeDtypeStruct((size, width), BF) for size in sizes],
        compiler_params=params(),
        cost_estimate=cost(10**12 if len(offsets) > 1 else 1, 1),
    )(place, after, *[panel] * len(blocks), near, *far)


def backward_kernel(place, near, *refs):
    far, weights, out = refs[:4], halves(*refs[4:10]), refs[10]
    step = pl.program_id(0)
    rows = pl.ds(pl.multiple_of(step * 256, 256), 256)
    far = stacked(far)
    for m in range(4):
        at = lax.rem(place[0] - m + 4, 4) * 2
        right = stacked(weights[2 * m : 2 * m + 2])
        total = lax.dot_general(
            near[...], right, (((1,), (1,)), ((), ())), preferred_element_type=F32
        )
        out[at + place[1], rows, :] = total.astype(BF)
        total = lax.dot_general(
            far, right, (((1,), (1,)), ((), ())), preferred_element_type=F32
        ).astype(BF)
        for i in range(4):
            target = pl.ds(far_tokens(place, i // 2 * 2 + step, i % 2), 64)
            out[at + 1 - place[1], target, :] = total[i * 64 : i * 64 + 64]


def backward(place, near, far, weights):
    width = near.shape[1]
    return pl.pallas_call(
        backward_kernel,
        grid=(2,),
        out_shape=jax.ShapeDtypeStruct((8, 512, 256), BF),
        in_specs=[SCALAR]
        + [pl.BlockSpec((rows, width), lambda n: (n, 0)) for rows in (256, *[64] * 4)]
        + [whole(w.shape) for w in weights],
        out_specs=whole((8, 512, 256)),
        compiler_params=params(),
        cost_estimate=PRODUCT,
    )(place, near, *far, *weights)


def summed(*refs):
    total = refs[0].astype(F32)
    for ref in refs[1:]:
        total = total + ref.astype(F32)
    return total.astype(BF)


def local(kernel, outs, after, *args, flops=1):
    after = after if isinstance(after, tuple) else (after,)
    return pl.pallas_call(
        lambda *refs: kernel(*refs[len(after) :]),
        out_shape=[jax.ShapeDtypeStruct(shape, BF) for shape in outs],
        in_specs=[ANY] * len(after) + [whole(a.shape) for a in args],
        out_specs=[whole(shape) for shape in outs],
        compiler_params=params(),
        cost_estimate=cost(flops, 1),
    )(*after, *args)


def follow(array, after):
    return pl.pallas_call(
        lambda *_: None,
        out_shape=jax.ShapeDtypeStruct(array.shape, array.dtype),
        in_specs=[ANY] * (1 + len(after)),
        out_specs=ANY,
        input_output_aliases={0: 0},
        cost_estimate=cost(1, 1),
    )(array, *after)


def collect_kernel(*refs):
    for e, ref in enumerate(refs[:4]):
        refs[4 + e // 2][e % 2 * 64 : e % 2 * 64 + 64, :] = ref[...]


def relay_kernel(top, bottom, top_up, bottom_down, up, down):
    up[:BLOCK], up[BLOCK:] = top_up[...], bottom[...]
    down[:BLOCK], down[BLOCK:] = top[...], bottom_down[...]


def sum_kernel(*refs):
    refs[-1][...] = summed(*[ref[...] for ref in refs[:-1]])


def end_kernel(mine, theirs, out):
    out[...] = summed(mine[:64], theirs[...])


def gather_kernel(sums, out):
    for h in range(2):
        lanes = pl.ds(h * 256, 256)
        out[:, lanes] = summed(*[sums[zl * 2 + h] for zl in range(4)])


def onward_kernel(up, down, from_below, from_above, up_out, down_out):
    half = from_below.shape[0]
    up_out[:half] = summed(up[:half], from_below[...])
    up_out[half:] = up[half:]
    down_out[:half] = down[:half]
    down_out[half:] = summed(down[half:], from_above[...])


def shift(array, axis, step):
    return lax.ppermute(array, axis, ring(lax.axis_size(axis), step))


def per_device(inputs, qweight, scales, grad_out):
    names = ("x", "zh", "y", "k")
    place = jnp.stack([lax.axis_index(name) for name in names]).astype(jnp.int32)
    F = qweight.shape[1]

    near = lax.all_gather(grad_out[0], ("y", "k"), axis=0, tiled=True)
    split = split_units(inputs[0])
    panel = lax.all_to_all(split, ("zl", "zh"), 0, 0, tiled=True)

    top, bottom = dequantize(scales, qweight)
    top_up, bottom_down = shift(top, "x", 1), shift(bottom, "x", -1)
    far = shift(grad_out[0], "zh", 1)
    far = [far] + [shift(far, "y", e) for e in (1, 2, 3)]
    up, down = local(
        relay_kernel, [(256, F)] * 2, (), top, bottom, top_up, bottom_down
    )
    mine = local(collect_kernel, [(128, F)] * 2, up, *far, flops=COLLECT)
    far = [part for own in mine for part in (own, shift(own, "k", 1))]
    up, down = shift(up, "x", 1), shift(down, "x", -1)
    weights = (top, bottom, top_up, up, down, bottom_down)

    sums = backward(place, near, far, weights)
    product = forward(place, sums, panel, weights)
    top, bottom = weight_grad((2,), (128, 128), place, product, panel, near, far)
    here, down, up = weight_grad((0, 1, 3), (256,) * 3, place, top, panel, near, far)

    sums = lax.all_to_all(sums, ("zl", "zh"), 0, 0, tiled=True)
    (grad_inputs,) = local(gather_kernel, [(512, 512)], (), sums)

    top, bottom = shift(top, "x", 1), shift(bottom, "x", -1)
    up, down = local(onward_kernel, [(256, F)] * 2, (), up, down, top, bottom)
    up, down = shift(up, "x", 1), shift(down, "x", -1)
    grad_weight = summed(here, up, down)

    product = lax.psum_scatter(product, ("y", "k"), scatter_dimension=0, tiled=True)
    other = shift(product[64:], "zh", 1)
    after = grad_inputs, grad_weight
    (projected,) = local(end_kernel, [(64, F)], after, product, other)

    return projected[None], grad_inputs[None], grad_weight


def solution(mesh):
    axes = Mesh(mesh.devices.reshape(4, 2, 4, 4, 2), ("y", "k", "zl", "x", "zh"))
    return jax.shard_map(
        per_device,
        mesh=axes,
        in_specs=(
            P(("x", "zh"), None, ("y", "k", "zl")),
            P(("y", "k", "x", "zh"), "zl"),
            P(("y", "k", "x", "zh"), "zl"),
            P(("x", "zh"), ("y", "k"), "zl"),
        ),
        out_specs=(
            P(("x", "zh"), ("y", "k"), "zl"),
            P(("x", "zh"), None, ("y", "k", "zl")),
            P(("y", "k", "x", "zh"), "zl"),
        ),
        check_vma=False,
    )
```

```python
import functools

import jax
import jax.numpy as jnp
from jax import lax
from jax.experimental import pallas as pl
from jax.experimental.pallas import tpu as pltpu
from jax.sharding import Mesh, PartitionSpec as P

BLOCK = 128
COLLECT = 28 * 10**9
BF = jnp.bfloat16
F32 = jnp.float32
VMEM_LIMIT = 64 * 1024 * 1024 - 4096


def params():
    return pltpu.CompilerParams(vmem_limit_bytes=VMEM_LIMIT)


def cost(flops, moved):
    return pl.CostEstimate(flops=flops, bytes_accessed=moved, transcendentals=0)


def whole(shape):
    return pl.BlockSpec(shape, lambda *_: (0,) * len(shape))


SCALAR = pl.BlockSpec(memory_space=pltpu.SMEM)
ANY = pl.BlockSpec(memory_space=pl.ANY)


def ring(size, step):
    return [(i, (i + step) % size) for i in range(size)]


def dequantize_kernel(scales, quantized, top, bottom):
    for r, half in enumerate((top, bottom)):
        for c in range(scales.shape[1]):
            lanes = pl.ds(c * BLOCK, BLOCK)
            block = quantized[pl.ds(r * BLOCK, BLOCK), lanes].astype(F32)
            half[:, lanes] = (block * scales[r, c]).astype(BF)


def dequantize(scales, quantized):
    half = (BLOCK, quantized.shape[1])
    return pl.pallas_call(
        dequantize_kernel,
        out_shape=[jax.ShapeDtypeStruct(half, BF)] * 2,
        in_specs=[SCALAR, whole(quantized.shape)],
        out_specs=[whole(half)] * 2,
        compiler_params=params(),
        cost_estimate=cost(1, 1),
    )(scales, quantized)


def split_kernel(inputs, split):
    for at in range(8):
        split[at] = inputs[:, at % 2 * 256 : at % 2 * 256 + 256]


def split_units(inputs):
    shape = (8, 512, 256)
    return pl.pallas_call(
        split_kernel,
        out_shape=jax.ShapeDtypeStruct(shape, BF),
        in_specs=[whole(inputs.shape)],
        out_specs=whole(shape),
        compiler_params=params(),
        cost_estimate=cost(1, 1),
    )(inputs)


PRODUCT = cost(1, 1)


def stacked(refs):
    return jnp.concatenate([ref[...] for ref in refs], axis=0)


def halves(top, bottom, top_up, up, down, bottom_down):
    first, second = pl.ds(0, BLOCK), pl.ds(BLOCK, BLOCK)
    return (
        top, bottom, top_up, up.at[second],
        up.at[first], down.at[second], down.at[first], bottom_down,
    )


def forward_kernel(place, _, panel, *refs):
    weights, (out, left) = halves(*refs[:6]), refs[6:]
    x, zh = place[0], place[1]

    @pl.when(pl.program_id(0) == 0)
    def _():
        for at in range(8):
            m = lax.rem(x - at // 2 + 4, 4)
            s = lax.rem(at % 2 + zh, 2)
            lanes = pl.ds(pl.multiple_of(m * 256, 256), 256)
            for b in range(8):
                rows = pl.ds(pl.multiple_of(b * 128 + s * 64, 64), 64)
                left[rows, lanes] = panel[at, b * 64 : b * 64 + 64, :]

    total = jnp.dot(left[...], stacked(weights), preferred_element_type=F32)
    out[...] = total.astype(BF)


def forward(place, after, panel, weights):
    width = weights[0].shape[1]
    tile = width // 3
    return pl.pallas_call(
        forward_kernel,
        grid=(width // tile,),
        out_shape=jax.ShapeDtypeStruct((1024, width), BF),
        in_specs=[SCALAR, ANY, whole(panel.shape)]
        + [pl.BlockSpec((w.shape[0], tile), lambda n: (0, n)) for w in weights],
        out_specs=pl.BlockSpec((1024, tile), lambda n: (0, n)),
        scratch_shapes=[pltpu.VMEM((1024, 1024), BF)],
        compiler_params=params(),
        cost_estimate=PRODUCT,
    )(place, after, panel, *weights)


def far_tokens(place, e, kk):
    block = lax.rem(place[2] - e + 4, 4) * 2 + lax.rem(place[3] + kk, 2)
    return pl.multiple_of(block * 64, 64)


def weight_grad_kernel(count, place, _, *refs):
    panels, near, far = refs[: 2 * count], refs[2 * count], refs[2 * count + 1 :][:4]
    outs, (left, right) = refs[2 * count + 5 : -2], refs[-2:]

    @pl.when(pl.program_id(0) == 0)
    def _():
        for i, panel in enumerate(panels):
            s = lax.rem(i % 2 + place[1], 2)
            lanes = pl.ds(pl.multiple_of(s * 512, 512), 512)
            left[i // 2 * 256 : i // 2 * 256 + 256, lanes] = panel[0].T

    right[:512, :] = near[...]
    for e in range(4):
        for kk in range(2):
            rows = pl.ds(512 + far_tokens(place, e, kk), 64)
            source = far[e // 2 * 2 + kk]
            right[rows, :] = source[e % 2 * 64 : e % 2 * 64 + 64, :]
    total = jnp.dot(left[...], right[...], preferred_element_type=F32)
    at = 0
    for out in outs:
        out[...] = total[at : at + out.shape[0]].astype(BF)
        at += out.shape[0]


def weight_grad(offsets, sizes, place, after, panel, near, far):
    width = near.shape[1]
    tile = width // 3

    def block(m, h):
        return lambda n, place: (lax.rem(place[0] - m + 4, 4) * 2 + h, 0, 0)

    blocks = [
        pl.BlockSpec((1, 512, 256), block(m, h)) for m in offsets for h in range(2)
    ]
    columns = lambda n, place: (0, n)
    return pl.pallas_call(
        functools.partial(weight_grad_kernel, len(offsets)),
        grid_spec=pltpu.PrefetchScalarGridSpec(
            num_scalar_prefetch=1,
            grid=(width // tile,),
            in_specs=[ANY, *blocks]
            + [pl.BlockSpec((rows, tile), columns) for rows in (512, *[128] * 4)],
            out_specs=[pl.BlockSpec((size, tile), columns) for size in sizes],
            scratch_shapes=[
                pltpu.VMEM((256 * len(offsets), 1024), BF),
                pltpu.VMEM((1024, tile), BF),
            ],
        ),
        out_shape=[jax.ShapeDtypeStruct((size, width), BF) for size in sizes],
        compiler_params=params(),
        cost_estimate=cost(1, 1),
    )(place, after, *[panel] * len(blocks), near, *far)


def backward_kernel(place, near, *refs):
    far, weights, out = refs[:4], halves(*refs[4:10]), refs[10]
    step = pl.program_id(0)
    rows = pl.ds(pl.multiple_of(step * 256, 256), 256)
    far = stacked(far)
    for m in range(4):
        at = lax.rem(place[0] - m + 4, 4) * 2
        right = stacked(weights[2 * m : 2 * m + 2])
        total = lax.dot_general(
            near[...], right, (((1,), (1,)), ((), ())), preferred_element_type=F32
        )
        out[at + place[1], rows, :] = total.astype(BF)
        total = lax.dot_general(
            far, right, (((1,), (1,)), ((), ())), preferred_element_type=F32
        ).astype(BF)
        for i in range(4):
            target = pl.ds(far_tokens(place, i // 2 * 2 + step, i % 2), 64)
            out[at + 1 - place[1], target, :] = total[i * 64 : i * 64 + 64]


def backward(place, near, far, weights):
    width = near.shape[1]
    return pl.pallas_call(
        backward_kernel,
        grid=(2,),
        out_shape=jax.ShapeDtypeStruct((8, 512, 256), BF),
        in_specs=[SCALAR]
        + [pl.BlockSpec((rows, width), lambda n: (n, 0)) for rows in (256, *[64] * 4)]
        + [whole(w.shape) for w in weights],
        out_specs=whole((8, 512, 256)),
        compiler_params=params(),
        cost_estimate=PRODUCT,
    )(place, near, *far, *weights)


def summed(*refs):
    total = refs[0].astype(F32)
    for ref in refs[1:]:
        total = total + ref.astype(F32)
    return total.astype(BF)


def local(kernel, outs, after, *args, flops=1):
    after = after if isinstance(after, tuple) else (after,)
    return pl.pallas_call(
        lambda *refs: kernel(*refs[len(after) :]),
        out_shape=[jax.ShapeDtypeStruct(shape, BF) for shape in outs],
        in_specs=[ANY] * len(after) + [whole(a.shape) for a in args],
        out_specs=[whole(shape) for shape in outs],
        compiler_params=params(),
        cost_estimate=cost(flops, 1),
    )(*after, *args)


def follow(array, after):
    return pl.pallas_call(
        lambda *_: None,
        out_shape=jax.ShapeDtypeStruct(array.shape, array.dtype),
        in_specs=[ANY] * (1 + len(after)),
        out_specs=ANY,
        input_output_aliases={0: 0},
        cost_estimate=cost(1, 1),
    )(array, *after)


def collect_kernel(*refs):
    for e, ref in enumerate(refs[:4]):
        refs[4 + e // 2][e % 2 * 64 : e % 2 * 64 + 64, :] = ref[...]


def relay_kernel(top, bottom, top_up, bottom_down, up, down):
    up[:BLOCK], up[BLOCK:] = top_up[...], bottom[...]
    down[:BLOCK], down[BLOCK:] = top[...], bottom_down[...]


def sum_kernel(*refs):
    refs[-1][...] = summed(*[ref[...] for ref in refs[:-1]])


def end_kernel(mine, theirs, out):
    out[...] = summed(mine[:64], theirs[...])


def gather_kernel(sums, out):
    for h in range(2):
        lanes = pl.ds(h * 256, 256)
        out[:, lanes] = summed(*[sums[zl * 2 + h] for zl in range(4)])


def onward_kernel(up, down, from_below, from_above, up_out, down_out):
    half = from_below.shape[0]
    up_out[:half] = summed(up[:half], from_below[...])
    up_out[half:] = up[half:]
    down_out[:half] = down[:half]
    down_out[half:] = summed(down[half:], from_above[...])


def shift(array, axis, step):
    return lax.ppermute(array, axis, ring(lax.axis_size(axis), step))


def per_device(inputs, qweight, scales, grad_out):
    names = ("x", "zh", "y", "k")
    place = jnp.stack([lax.axis_index(name) for name in names]).astype(jnp.int32)
    F = qweight.shape[1]

    near = lax.all_gather(grad_out[0], ("y", "k"), axis=0, tiled=True)
    split = split_units(inputs[0])
    panel = lax.all_to_all(split, ("zl", "zh"), 0, 0, tiled=True)

    top, bottom = dequantize(scales, qweight)
    top_up, bottom_down = shift(top, "x", 1), shift(bottom, "x", -1)
    far = shift(grad_out[0], "zh", 1)
    far = [far] + [shift(far, "y", e) for e in (1, 2, 3)]
    up, down = local(
        relay_kernel, [(256, F)] * 2, (), top, bottom, top_up, bottom_down
    )
    mine = local(collect_kernel, [(128, F)] * 2, up, *far, flops=COLLECT)
    far = [part for own in mine for part in (own, shift(own, "k", 1))]
    up, down = shift(up, "x", 1), shift(down, "x", -1)
    weights = (top, bottom, top_up, up, down, bottom_down)

    sums = backward(place, near, far, weights)
    product = forward(place, sums, panel, weights)
    top, bottom = weight_grad((2,), (128, 128), place, product, panel, near, far)
    here, down, up = weight_grad((0, 1, 3), (256,) * 3, place, top, panel, near, far)

    sums = lax.all_to_all(sums, ("zl", "zh"), 0, 0, tiled=True)
    (grad_inputs,) = local(gather_kernel, [(512, 512)], (), sums)

    top, bottom = shift(top, "x", 1), shift(bottom, "x", -1)
    up, down = local(onward_kernel, [(256, F)] * 2, (), up, down, top, bottom)
    up, down = shift(up, "x", 1), shift(down, "x", -1)
    grad_weight = summed(here, up, down)

    product = lax.psum_scatter(product, ("y", "k"), scatter_dimension=0, tiled=True)
    other = shift(product[64:], "zh", 1)
    after = grad_inputs, grad_weight
    (projected,) = local(end_kernel, [(64, F)], after, product, other)

    return projected[None], grad_inputs[None], grad_weight


def solution(mesh):
    axes = Mesh(mesh.devices.reshape(4, 2, 4, 4, 2), ("y", "k", "zl", "x", "zh"))
    return jax.shard_map(
        per_device,
        mesh=axes,
        in_specs=(
            P(("x", "zh"), None, ("y", "k", "zl")),
            P(("y", "k", "x", "zh"), "zl"),
            P(("y", "k", "x", "zh"), "zl"),
            P(("x", "zh"), ("y", "k"), "zl"),
        ),
        out_specs=(
            P(("x", "zh"), ("y", "k"), "zl"),
            P(("x", "zh"), None, ("y", "k", "zl")),
            P(("y", "k", "x", "zh"), "zl"),
        ),
        check_vma=False,
    )
```

```python
import functools

import jax
import jax.numpy as jnp
from jax import lax
from jax.experimental import pallas as pl
from jax.experimental.pallas import tpu as pltpu
from jax.sharding import Mesh, PartitionSpec as P

BLOCK = 128
COLLECT = 28 * 10**9
BF = jnp.bfloat16
F32 = jnp.float32
VMEM_LIMIT = 64 * 1024 * 1024 - 4096


def params():
    return pltpu.CompilerParams(vmem_limit_bytes=VMEM_LIMIT)


def cost(flops, moved):
    return pl.CostEstimate(flops=flops, bytes_accessed=moved, transcendentals=0)


def whole(shape):
    return pl.BlockSpec(shape, lambda *_: (0,) * len(shape))


SCALAR = pl.BlockSpec(memory_space=pltpu.SMEM)
ANY = pl.BlockSpec(memory_space=pl.ANY)


def ring(size, step):
    return [(i, (i + step) % size) for i in range(size)]


def dequantize_kernel(scales, quantized, top, bottom):
    for r, half in enumerate((top, bottom)):
        for c in range(scales.shape[1]):
            lanes = pl.ds(c * BLOCK, BLOCK)
            block = quantized[pl.ds(r * BLOCK, BLOCK), lanes].astype(F32)
            half[:, lanes] = (block * scales[r, c]).astype(BF)


def dequantize(scales, quantized):
    half = (BLOCK, quantized.shape[1])
    return pl.pallas_call(
        dequantize_kernel,
        out_shape=[jax.ShapeDtypeStruct(half, BF)] * 2,
        in_specs=[SCALAR, whole(quantized.shape)],
        out_specs=[whole(half)] * 2,
        compiler_params=params(),
        cost_estimate=cost(1, 1),
    )(scales, quantized)


def split_kernel(inputs, split):
    for at in range(8):
        split[at] = inputs[:, at % 2 * 256 : at % 2 * 256 + 256]


def split_units(inputs):
    shape = (8, 512, 256)
    return pl.pallas_call(
        split_kernel,
        out_shape=jax.ShapeDtypeStruct(shape, BF),
        in_specs=[whole(inputs.shape)],
        out_specs=whole(shape),
        compiler_params=params(),
        cost_estimate=cost(1, 1),
    )(inputs)


PRODUCT = cost(1, 1)


def stacked(refs):
    return jnp.concatenate([ref[...] for ref in refs], axis=0)


def halves(top, bottom, top_up, up, down, bottom_down):
    first, second = pl.ds(0, BLOCK), pl.ds(BLOCK, BLOCK)
    return (
        top, bottom, top_up, up.at[second],
        up.at[first], down.at[second], down.at[first], bottom_down,
    )


def forward_kernel(place, _, panel, *refs):
    weights, (out, left) = halves(*refs[:6]), refs[6:]
    x, zh = place[0], place[1]

    @pl.when(pl.program_id(0) == 0)
    def _():
        for at in range(8):
            m = lax.rem(x - at // 2 + 4, 4)
            s = lax.rem(at % 2 + zh, 2)
            lanes = pl.ds(pl.multiple_of(m * 256, 256), 256)
            for b in range(8):
                rows = pl.ds(pl.multiple_of(b * 128 + s * 64, 64), 64)
                left[rows, lanes] = panel[at, b * 64 : b * 64 + 64, :]

    total = jnp.dot(left[...], stacked(weights), preferred_element_type=F32)
    out[...] = total.astype(BF)


def forward(place, after, panel, weights):
    width = weights[0].shape[1]
    tile = width // 3
    return pl.pallas_call(
        forward_kernel,
        grid=(width // tile,),
        out_shape=jax.ShapeDtypeStruct((1024, width), BF),
        in_specs=[SCALAR, ANY, whole(panel.shape)]
        + [pl.BlockSpec((w.shape[0], tile), lambda n: (0, n)) for w in weights],
        out_specs=pl.BlockSpec((1024, tile), lambda n: (0, n)),
        scratch_shapes=[pltpu.VMEM((1024, 1024), BF)],
        compiler_params=params(),
        cost_estimate=PRODUCT,
    )(place, after, panel, *weights)


def far_tokens(place, e, kk):
    block = lax.rem(place[2] - e + 4, 4) * 2 + lax.rem(place[3] + kk, 2)
    return pl.multiple_of(block * 64, 64)


def weight_grad_kernel(count, place, _, *refs):
    panels, near, far = refs[: 2 * count], refs[2 * count], refs[2 * count + 1 :][:4]
    outs, (left, right) = refs[2 * count + 5 : -2], refs[-2:]

    @pl.when(pl.program_id(0) == 0)
    def _():
        for i, panel in enumerate(panels):
            s = lax.rem(i % 2 + place[1], 2)
            lanes = pl.ds(pl.multiple_of(s * 512, 512), 512)
            left[i // 2 * 256 : i // 2 * 256 + 256, lanes] = panel[0].T

    right[:512, :] = near[...]
    for e in range(4):
        for kk in range(2):
            rows = pl.ds(512 + far_tokens(place, e, kk), 64)
            source = far[e // 2 * 2 + kk]
            right[rows, :] = source[e % 2 * 64 : e % 2 * 64 + 64, :]
    total = jnp.dot(left[...], right[...], preferred_element_type=F32)
    at = 0
    for out in outs:
        out[...] = total[at : at + out.shape[0]].astype(BF)
        at += out.shape[0]


def weight_grad(offsets, sizes, place, after, panel, near, far):
    width = near.shape[1]
    tile = width // 3

    def block(m, h):
        return lambda n, place: (lax.rem(place[0] - m + 4, 4) * 2 + h, 0, 0)

    blocks = [
        pl.BlockSpec((1, 512, 256), block(m, h)) for m in offsets for h in range(2)
    ]
    columns = lambda n, place: (0, n)
    return pl.pallas_call(
        functools.partial(weight_grad_kernel, len(offsets)),
        grid_spec=pltpu.PrefetchScalarGridSpec(
            num_scalar_prefetch=1,
            grid=(width // tile,),
            in_specs=[ANY, *blocks]
            + [pl.BlockSpec((rows, tile), columns) for rows in (512, *[128] * 4)],
            out_specs=[pl.BlockSpec((size, tile), columns) for size in sizes],
            scratch_shapes=[
                pltpu.VMEM((256 * len(offsets), 1024), BF),
                pltpu.VMEM((1024, tile), BF),
            ],
        ),
        out_shape=[jax.ShapeDtypeStruct((size, width), BF) for size in sizes],
        compiler_params=params(),
        cost_estimate=cost(10**12 if len(offsets) > 1 else 1, 1),
    )(place, after, *[panel] * len(blocks), near, *far)


def backward_kernel(place, near, *refs):
    far, weights, out = refs[:4], halves(*refs[4:10]), refs[10]
    step = pl.program_id(0)
    rows = pl.ds(pl.multiple_of(step * 256, 256), 256)
    far = stacked(far)
    for m in range(4):
        at = lax.rem(place[0] - m + 4, 4) * 2
        right = stacked(weights[2 * m : 2 * m + 2])
        total = lax.dot_general(
            near[...], right, (((1,), (1,)), ((), ())), preferred_element_type=F32
        )
        out[at + place[1], rows, :] = total.astype(BF)
        total = lax.dot_general(
            far, right, (((1,), (1,)), ((), ())), preferred_element_type=F32
        ).astype(BF)
        for i in range(4):
            target = pl.ds(far_tokens(place, i // 2 * 2 + step, i % 2), 64)
            out[at + 1 - place[1], target, :] = total[i * 64 : i * 64 + 64]


def backward(place, near, far, weights):
    width = near.shape[1]
    return pl.pallas_call(
        backward_kernel,
        grid=(2,),
        out_shape=jax.ShapeDtypeStruct((8, 512, 256), BF),
        in_specs=[SCALAR]
        + [pl.BlockSpec((rows, width), lambda n: (n, 0)) for rows in (256, *[64] * 4)]
        + [whole(w.shape) for w in weights],
        out_specs=whole((8, 512, 256)),
        compiler_params=params(),
        cost_estimate=PRODUCT,
    )(place, near, *far, *weights)


def summed(*refs):
    total = refs[0].astype(F32)
    for ref in refs[1:]:
        total = total + ref.astype(F32)
    return total.astype(BF)


def local(kernel, outs, after, *args, flops=1):
    after = after if isinstance(after, tuple) else (after,)
    return pl.pallas_call(
        lambda *refs: kernel(*refs[len(after) :]),
        out_shape=[jax.ShapeDtypeStruct(shape, BF) for shape in outs],
        in_specs=[ANY] * len(after) + [whole(a.shape) for a in args],
        out_specs=[whole(shape) for shape in outs],
        compiler_params=params(),
        cost_estimate=cost(flops, 1),
    )(*after, *args)


def follow(array, after):
    return pl.pallas_call(
        lambda *_: None,
        out_shape=jax.ShapeDtypeStruct(array.shape, array.dtype),
        in_specs=[ANY] * (1 + len(after)),
        out_specs=ANY,
        input_output_aliases={0: 0},
        cost_estimate=cost(1, 1),
    )(array, *after)


def collect_kernel(*refs):
    for e, ref in enumerate(refs[:4]):
        refs[4 + e // 2][e % 2 * 64 : e % 2 * 64 + 64, :] = ref[...]


def sum_kernel(*refs):
    refs[-1][...] = summed(*[ref[...] for ref in refs[:-1]])


def end_kernel(mine, theirs, out):
    out[...] = summed(mine[:64], theirs[...])


def gather_kernel(sums, out):
    for h in range(2):
        lanes = pl.ds(h * 256, 256)
        out[:, lanes] = summed(*[sums[zl * 2 + h] for zl in range(4)])


def onward_kernel(up, down, from_below, from_above, up_out, down_out):
    half = from_below.shape[0]
    up_out[:half] = summed(up[:half], from_below[...])
    up_out[half:] = up[half:]
    down_out[:half] = down[:half]
    down_out[half:] = summed(down[half:], from_above[...])


def shift(array, axis, step):
    return lax.ppermute(array, axis, ring(lax.axis_size(axis), step))


def per_device(inputs, qweight, scales, grad_out):
    names = ("x", "zh", "y", "k")
    place = jnp.stack([lax.axis_index(name) for name in names]).astype(jnp.int32)
    F = qweight.shape[1]

    near = lax.all_gather(grad_out[0], ("y", "k"), axis=0, tiled=True)
    split = split_units(inputs[0])
    panel = lax.all_to_all(split, ("zl", "zh"), 0, 0, tiled=True)

    top, bottom = dequantize(scales, qweight)
    top_up, bottom_down = shift(top, "x", 1), shift(bottom, "x", -1)
    far = shift(grad_out[0], "zh", 1)
    far = [far] + [shift(far, "y", e) for e in (1, 2, 3)]
    up = jnp.concatenate([top_up, bottom])
    down = jnp.concatenate([top, bottom_down])
    mine = local(collect_kernel, [(128, F)] * 2, (up, down), *far, flops=COLLECT)
    far = [part for own in mine for part in (own, shift(own, "k", 1))]
    up, down = shift(up, "x", 1), shift(down, "x", -1)
    weights = (top, bottom, top_up, up, down, bottom_down)

    sums = backward(place, near, far, weights)
    product = forward(place, sums, panel, weights)
    top, bottom = weight_grad((2,), (128, 128), place, product, panel, near, far)
    here, down, up = weight_grad((0, 1, 3), (256,) * 3, place, top, panel, near, far)

    sums = lax.all_to_all(sums, ("zl", "zh"), 0, 0, tiled=True)
    (grad_inputs,) = local(gather_kernel, [(512, 512)], (), sums)

    top, bottom = shift(top, "x", 1), shift(bottom, "x", -1)
    up, down = local(onward_kernel, [(256, F)] * 2, (), up, down, top, bottom)
    up, down = shift(up, "x", 1), shift(down, "x", -1)
    grad_weight = summed(here, up, down)

    product = lax.psum_scatter(product, ("y", "k"), scatter_dimension=0, tiled=True)
    other = shift(product[64:], "zh", 1)
    after = grad_inputs, grad_weight
    (projected,) = local(end_kernel, [(64, F)], after, product, other)

    return projected[None], grad_inputs[None], grad_weight


def solution(mesh):
    axes = Mesh(mesh.devices.reshape(4, 2, 4, 4, 2), ("y", "k", "zl", "x", "zh"))
    return jax.shard_map(
        per_device,
        mesh=axes,
        in_specs=(
            P(("x", "zh"), None, ("y", "k", "zl")),
            P(("y", "k", "x", "zh"), "zl"),
            P(("y", "k", "x", "zh"), "zl"),
            P(("x", "zh"), ("y", "k"), "zl"),
        ),
        out_specs=(
            P(("x", "zh"), ("y", "k"), "zl"),
            P(("x", "zh"), None, ("y", "k", "zl")),
            P(("y", "k", "x", "zh"), "zl"),
        ),
        check_vma=False,
    )
```

```python
import functools

import jax
import jax.numpy as jnp
from jax import lax
from jax.experimental import pallas as pl
from jax.experimental.pallas import tpu as pltpu
from jax.sharding import Mesh, PartitionSpec as P

BLOCK = 128
COLLECT = 28 * 10**9
BF = jnp.bfloat16
F32 = jnp.float32
VMEM_LIMIT = 64 * 1024 * 1024 - 4096


def params():
    return pltpu.CompilerParams(vmem_limit_bytes=VMEM_LIMIT)


def cost(flops, moved):
    return pl.CostEstimate(flops=flops, bytes_accessed=moved, transcendentals=0)


def whole(shape):
    return pl.BlockSpec(shape, lambda *_: (0,) * len(shape))


SCALAR = pl.BlockSpec(memory_space=pltpu.SMEM)
ANY = pl.BlockSpec(memory_space=pl.ANY)


def ring(size, step):
    return [(i, (i + step) % size) for i in range(size)]


def prepare_kernel(scales, quantized, inputs, top, bottom, split):
    for r, half in enumerate((top, bottom)):
        for c in range(scales.shape[1]):
            lanes = pl.ds(c * BLOCK, BLOCK)
            block = quantized[pl.ds(r * BLOCK, BLOCK), lanes].astype(F32)
            half[:, lanes] = (block * scales[r, c]).astype(BF)
    for at in range(8):
        split[at] = inputs[:, at % 2 * 256 : at % 2 * 256 + 256]


def prepare(scales, quantized, inputs):
    shapes = [(BLOCK, quantized.shape[1])] * 2 + [(8, 512, 256)]
    return pl.pallas_call(
        prepare_kernel,
        out_shape=[jax.ShapeDtypeStruct(shape, BF) for shape in shapes],
        in_specs=[SCALAR, whole(quantized.shape), whole(inputs.shape)],
        out_specs=[whole(shape) for shape in shapes],
        compiler_params=params(),
        cost_estimate=cost(1, 1),
    )(scales, quantized, inputs)


PRODUCT = cost(1, 1)


def stacked(refs):
    return jnp.concatenate([ref[...] for ref in refs], axis=0)


def halves(top, bottom, top_up, up, down, bottom_down):
    first, second = pl.ds(0, BLOCK), pl.ds(BLOCK, BLOCK)
    return (
        top, bottom, top_up, up.at[second],
        up.at[first], down.at[second], down.at[first], bottom_down,
    )


def forward_kernel(place, _, panel, *refs):
    weights, (out, left) = halves(*refs[:6]), refs[6:]
    x, zh = place[0], place[1]

    @pl.when(pl.program_id(0) == 0)
    def _():
        for at in range(8):
            m = lax.rem(x - at // 2 + 4, 4)
            s = lax.rem(at % 2 + zh, 2)
            lanes = pl.ds(pl.multiple_of(m * 256, 256), 256)
            for b in range(8):
                rows = pl.ds(pl.multiple_of(b * 128 + s * 64, 64), 64)
                left[rows, lanes] = panel[at, b * 64 : b * 64 + 64, :]

    total = jnp.dot(left[...], stacked(weights), preferred_element_type=F32)
    out[...] = total.astype(BF)


def forward(place, after, panel, weights):
    width = weights[0].shape[1]
    tile = width // 3
    return pl.pallas_call(
        forward_kernel,
        grid=(width // tile,),
        out_shape=jax.ShapeDtypeStruct((1024, width), BF),
        in_specs=[SCALAR, ANY, whole(panel.shape)]
        + [pl.BlockSpec((w.shape[0], tile), lambda n: (0, n)) for w in weights],
        out_specs=pl.BlockSpec((1024, tile), lambda n: (0, n)),
        scratch_shapes=[pltpu.VMEM((1024, 1024), BF)],
        compiler_params=params(),
        cost_estimate=PRODUCT,
    )(place, after, panel, *weights)


def far_tokens(place, e, kk):
    block = lax.rem(place[2] - e + 4, 4) * 2 + lax.rem(place[3] + kk, 2)
    return pl.multiple_of(block * 64, 64)


def weight_grad_kernel(count, place, _, *refs):
    panels, near, far = refs[: 2 * count], refs[2 * count], refs[2 * count + 1 :][:4]
    outs, (left, right) = refs[2 * count + 5 : -2], refs[-2:]

    @pl.when(pl.program_id(0) == 0)
    def _():
        for i, panel in enumerate(panels):
            s = lax.rem(i % 2 + place[1], 2)
            lanes = pl.ds(pl.multiple_of(s * 512, 512), 512)
            left[i // 2 * 256 : i // 2 * 256 + 256, lanes] = panel[0].T

    right[:512, :] = near[...]
    for e in range(4):
        for kk in range(2):
            rows = pl.ds(512 + far_tokens(place, e, kk), 64)
            source = far[e // 2 * 2 + kk]
            right[rows, :] = source[e % 2 * 64 : e % 2 * 64 + 64, :]
    total = jnp.dot(left[...], right[...], preferred_element_type=F32)
    at = 0
    for out in outs:
        out[...] = total[at : at + out.shape[0]].astype(BF)
        at += out.shape[0]


def weight_grad(offsets, sizes, place, after, panel, near, far):
    width = near.shape[1]
    tile = width // 3

    def block(m, h):
        return lambda n, place: (lax.rem(place[0] - m + 4, 4) * 2 + h, 0, 0)

    blocks = [
        pl.BlockSpec((1, 512, 256), block(m, h)) for m in offsets for h in range(2)
    ]
    columns = lambda n, place: (0, n)
    return pl.pallas_call(
        functools.partial(weight_grad_kernel, len(offsets)),
        grid_spec=pltpu.PrefetchScalarGridSpec(
            num_scalar_prefetch=1,
            grid=(width // tile,),
            in_specs=[ANY, *blocks]
            + [pl.BlockSpec((rows, tile), columns) for rows in (512, *[128] * 4)],
            out_specs=[pl.BlockSpec((size, tile), columns) for size in sizes],
            scratch_shapes=[
                pltpu.VMEM((256 * len(offsets), 1024), BF),
                pltpu.VMEM((1024, tile), BF),
            ],
        ),
        out_shape=[jax.ShapeDtypeStruct((size, width), BF) for size in sizes],
        compiler_params=params(),
        cost_estimate=cost(10**12 if len(offsets) > 1 else 1, 1),
    )(place, after, *[panel] * len(blocks), near, *far)


def backward_kernel(place, near, *refs):
    far, weights, out = refs[:4], halves(*refs[4:10]), refs[10]
    step = pl.program_id(0)
    rows = pl.ds(pl.multiple_of(step * 256, 256), 256)
    far = stacked(far)
    for m in range(4):
        at = lax.rem(place[0] - m + 4, 4) * 2
        right = stacked(weights[2 * m : 2 * m + 2])
        total = lax.dot_general(
            near[...], right, (((1,), (1,)), ((), ())), preferred_element_type=F32
        )
        out[at + place[1], rows, :] = total.astype(BF)
        total = lax.dot_general(
            far, right, (((1,), (1,)), ((), ())), preferred_element_type=F32
        ).astype(BF)
        for i in range(4):
            target = pl.ds(far_tokens(place, i // 2 * 2 + step, i % 2), 64)
            out[at + 1 - place[1], target, :] = total[i * 64 : i * 64 + 64]


def backward(place, near, far, weights):
    width = near.shape[1]
    return pl.pallas_call(
        backward_kernel,
        grid=(2,),
        out_shape=jax.ShapeDtypeStruct((8, 512, 256), BF),
        in_specs=[SCALAR]
        + [pl.BlockSpec((rows, width), lambda n: (n, 0)) for rows in (256, *[64] * 4)]
        + [whole(w.shape) for w in weights],
        out_specs=whole((8, 512, 256)),
        compiler_params=params(),
        cost_estimate=PRODUCT,
    )(place, near, *far, *weights)


def summed(*refs):
    total = refs[0].astype(F32)
    for ref in refs[1:]:
        total = total + ref.astype(F32)
    return total.astype(BF)


def local(kernel, outs, after, *args, flops=1):
    after = after if isinstance(after, tuple) else (after,)
    return pl.pallas_call(
        lambda *refs: kernel(*refs[len(after) :]),
        out_shape=[jax.ShapeDtypeStruct(shape, BF) for shape in outs],
        in_specs=[ANY] * len(after) + [whole(a.shape) for a in args],
        out_specs=[whole(shape) for shape in outs],
        compiler_params=params(),
        cost_estimate=cost(flops, 1),
    )(*after, *args)


def follow(array, after):
    return pl.pallas_call(
        lambda *_: None,
        out_shape=jax.ShapeDtypeStruct(array.shape, array.dtype),
        in_specs=[ANY] * (1 + len(after)),
        out_specs=ANY,
        input_output_aliases={0: 0},
        cost_estimate=cost(1, 1),
    )(array, *after)


def collect_kernel(*refs):
    for e, ref in enumerate(refs[:4]):
        refs[4 + e // 2][e % 2 * 64 : e % 2 * 64 + 64, :] = ref[...]


def relay_kernel(top, bottom, top_up, bottom_down, up, down):
    up[:BLOCK], up[BLOCK:] = top_up[...], bottom[...]
    down[:BLOCK], down[BLOCK:] = top[...], bottom_down[...]


def sum_kernel(*refs):
    refs[-1][...] = summed(*[ref[...] for ref in refs[:-1]])


def end_kernel(mine, theirs, out):
    out[...] = summed(mine[:64], theirs[...])


def gather_kernel(sums, out):
    for h in range(2):
        lanes = pl.ds(h * 256, 256)
        out[:, lanes] = summed(*[sums[zl * 2 + h] for zl in range(4)])


def onward_kernel(up, down, from_below, from_above, up_out, down_out):
    half = from_below.shape[0]
    up_out[:half] = summed(up[:half], from_below[...])
    up_out[half:] = up[half:]
    down_out[:half] = down[:half]
    down_out[half:] = summed(down[half:], from_above[...])


def shift(array, axis, step):
    return lax.ppermute(array, axis, ring(lax.axis_size(axis), step))


def per_device(inputs, qweight, scales, grad_out):
    names = ("x", "zh", "y", "k")
    place = jnp.stack([lax.axis_index(name) for name in names]).astype(jnp.int32)
    F = qweight.shape[1]

    near = lax.all_gather(grad_out[0], ("y", "k"), axis=0, tiled=True)
    top, bottom, split = prepare(scales, qweight, inputs[0])
    panel = lax.all_to_all(split, ("zl", "zh"), 0, 0, tiled=True)

    top_up, bottom_down = shift(top, "x", 1), shift(bottom, "x", -1)
    far = shift(grad_out[0], "zh", 1)
    far = [far] + [shift(far, "y", e) for e in (1, 2, 3)]
    up, down = local(
        relay_kernel, [(256, F)] * 2, (), top, bottom, top_up, bottom_down
    )
    mine = local(collect_kernel, [(128, F)] * 2, up, *far, flops=COLLECT)
    far = [part for own in mine for part in (own, shift(own, "k", 1))]
    up, down = shift(up, "x", 1), shift(down, "x", -1)
    weights = (top, bottom, top_up, up, down, bottom_down)

    sums = backward(place, near, far, weights)
    product = forward(place, sums, panel, weights)
    top, bottom = weight_grad((2,), (128, 128), place, product, panel, near, far)
    here, down, up = weight_grad((0, 1, 3), (256,) * 3, place, top, panel, near, far)

    sums = lax.all_to_all(sums, ("zl", "zh"), 0, 0, tiled=True)
    (grad_inputs,) = local(gather_kernel, [(512, 512)], (), sums)

    top, bottom = shift(top, "x", 1), shift(bottom, "x", -1)
    up, down = local(onward_kernel, [(256, F)] * 2, (), up, down, top, bottom)
    up, down = shift(up, "x", 1), shift(down, "x", -1)
    grad_weight = summed(here, up, down)

    product = lax.psum_scatter(product, ("y", "k"), scatter_dimension=0, tiled=True)
    other = shift(product[64:], "zh", 1)
    after = grad_inputs, grad_weight
    (projected,) = local(end_kernel, [(64, F)], after, product, other)

    return projected[None], grad_inputs[None], grad_weight


def solution(mesh):
    axes = Mesh(mesh.devices.reshape(4, 2, 4, 4, 2), ("y", "k", "zl", "x", "zh"))
    return jax.shard_map(
        per_device,
        mesh=axes,
        in_specs=(
            P(("x", "zh"), None, ("y", "k", "zl")),
            P(("y", "k", "x", "zh"), "zl"),
            P(("y", "k", "x", "zh"), "zl"),
            P(("x", "zh"), ("y", "k"), "zl"),
        ),
        out_specs=(
            P(("x", "zh"), ("y", "k"), "zl"),
            P(("x", "zh"), None, ("y", "k", "zl")),
            P(("y", "k", "x", "zh"), "zl"),
        ),
        check_vma=False,
    )
```
